32 devices in a mesh: row: 8 (over z, core), col: 4 (over y, x).
Axes of the slice: x: 2, y: 2, z: 4, core: 2. Of those that a mesh axis runs over, the one named last changes fastest.
Arguments:
- density: float32 [96, 13, 128, 128], P('row', None, 'col'), may hold values from -1.5 to 1.5
- pattern: int32 [96, 13], P('row'), may hold values from 0 to 1, as said below
Outputs:
- purified: float32 [96, 13, 128, 128], P('row', None, 'col')
The draws below stay inside these ranges and needn't reach their ends.
Inputs may be any that keep to these rules, and one draw needn't show every extreme that they name: `pattern`: each block row has exactly 7 ones, placed at random slots.
All inputs are finite; a program needn't handle non-finite values.
Results may differ from the reference program's by a relative error of at most 0.0003.
Values sent between devices are 32-bit elements; how exact they have to be, the bound alone decides.
A program may use at most 64 MiB of HBM per device.

```python
import jax
import jax.numpy as jnp
from jax import lax

B = 128
K = 13
NZ = 7
NBLK = 96


def one_order(row_key):
    return jax.random.permutation(row_key, K)


def draw_pattern(key, part):
    key = jax.random.fold_in(key, 7)
    row_keys = jax.random.split(key, NBLK)
    orders = jax.vmap(one_order)(row_keys)
    return (orders < NZ).astype(jnp.int32)


def shard_levels(stream_key, shape, cuts, least, high):
    def one(axis_at, blocks):
        steps = jax.random.uniform(jax.random.fold_in(jax.random.fold_in(stream_key, 6), axis_at), (blocks,), jnp.float32, least / len(cuts), high / len(cuts))
        return jnp.repeat(jnp.exp(steps), shape[axis_at] // blocks).reshape((-1,) + (1,) * (len(shape) - axis_at - 1))

    level = one(*cuts[0])
    for cut in cuts[1:]:
        level = level * one(*cut)
    return level


def noise(rng, shape, spread, reach, shards=(), held_as=jnp.bfloat16):
    entries = jax.random.normal(rng, shape, jnp.float32) * spread
    if len(shards) > 0:
        entries = shard_levels(rng, shape, shards, -0.22, 0.18) * entries
    return jnp.clip(entries, min=-reach, max=reach).astype(held_as)


def setup_inputs(seed: int = 0) -> dict:
    keys = jax.random.split(jax.random.key(seed), 3)
    density = noise(keys[0], (NBLK, K, B, B), 0.1, 1.5, ((0, 8), (2, 4)), jnp.float32)
    pattern = draw_pattern(jax.random.fold_in(keys[2], 71), 0)
    return dict(density=density, pattern=pattern)


def reference(density, pattern):
    total_rows, band_slots, block_size, _ = density.shape
    half_band = (band_slots - 1) // 2
    span_slots = 2 * band_slots - 1
    masked = jnp.swapaxes(density * pattern[:, :, None, None].astype(jnp.float32), 2, 3)
    slot_range = jnp.arange(band_slots, dtype=jnp.int32)
    slot_place = ((slot_range[:, None] + slot_range[None, :])[:, :, None] == jnp.arange(span_slots, dtype=jnp.int32)[None, None, :]).astype(jnp.float32)
    columns = 2 * half_band - slot_range[:, None] + slot_range[None, :]

    def square_row(row_index):
        near_rows = (row_index + slot_range - half_band) % total_rows
        products = jnp.einsum('sac,sdcb->sdab', masked[row_index], masked[near_rows], precision=lax.Precision.HIGHEST)
        return jnp.einsum('sdab,sde->eab', products, slot_place, precision=lax.Precision.HIGHEST)

    square = lax.map(square_row, jnp.arange(total_rows, dtype=jnp.int32))

    def cube_row(row_index):
        near_rows = (row_index + slot_range - half_band) % total_rows
        right_blocks = square[near_rows[:, None], columns]
        return jnp.einsum('sac,sicb->iab', masked[row_index], right_blocks, precision=lax.Precision.HIGHEST)

    third_power = lax.map(cube_row, jnp.arange(total_rows, dtype=jnp.int32))
    band_core = square[:, half_band:half_band + band_slots]
    result = (3.0 * band_core - 2.0 * third_power) * pattern[:, :, None, None].astype(jnp.float32)
    return jnp.swapaxes(result, 2, 3)
```

```python
import functools

import jax
import jax.numpy as jnp
from jax import lax
from jax.experimental import pallas as pl
from jax.experimental.pallas import tpu as pltpu
from jax.sharding import PartitionSpec as P

NZ = 7
MESH = pl.DeviceIdType.MESH


def split(x):
    hi = x.astype(jnp.bfloat16)
    return hi, (x - hi.astype(jnp.float32)).astype(jnp.bfloat16)


def dot3(lhi, llo, rhi, rlo):
    f = functools.partial(jnp.dot, preferred_element_type=jnp.float32)
    return f(lhi, rhi) + f(lhi, rlo) + f(llo, rhi)


def kernel(n_row, n_col, d_ref, pat, rank, slots, out, *scratch):
    panels = scratch[:6]
    (mext, lhi, llo, rhi, rlo, sx, shi, slo, acc, m_send, m_recv, s_send, s_recv,
     p_send, p_recv, f_send, f_recv) = scratch[6:]
    w = d_ref.shape[2]
    band = d_ref.shape[1]
    half = (band - 1) // 2
    steps = half + 1
    nb = d_ref.shape[3]
    wide = 2 * nb
    tall = (band + 1) * w
    row = lax.axis_index("row")
    col = lax.axis_index("col")
    odd = lax.rem(row, 2)
    left = lax.rem(row + n_row - 1, n_row)
    right = lax.rem(row + 1, n_row)
    outer = left + odd * (right - left)
    mate = row + 1 - 2 * odd
    grid2 = n_col == 4
    if grid2:
        xn = col + 1 - 2 * lax.rem(col, 2)
        yn = lax.rem(col + 2, 4)
        peers = [xn, yn]
    else:
        peers = [lax.rem(col + d, n_col) for d in range(1, n_col)]

    def pair(q):
        if q < 3:
            return (2 - q) + odd * (1 + 2 * q)
        return q + odd * (5 - 2 * q)

    def faces_right(q):
        return odd if q < 3 else 1 - odd

    def nbr(q):
        return outer if q < 3 else mate

    def landed(q):
        p = 5 - pair(q)
        return lax.rem(p + 9, 12)

    barrier = pltpu.get_barrier_semaphore()
    for peer in peers:
        pl.semaphore_signal(barrier, inc=1, device_id=(row, peer), device_id_type=MESH)
    for peer in (left, right):
        pl.semaphore_signal(barrier, inc=1, device_id=(peer, col), device_id_type=MESH)

    for q in range(6):
        p = pair(q)
        for dr in range(2):
            r = 2 * p + dr
            for s in range(band):
                mext[3 + p, dr, s] = d_ref[r, s] * pat[r, s].astype(jnp.float32)
            for t in range(NZ):
                panels[q][col, dr, t] = d_ref[r, slots[r, t]]

    pl.semaphore_wait(barrier, len(peers) + 2)

    def m_copy(q):
        p = pair(q)
        return pltpu.make_async_remote_copy(
            mext.at[3 + p], mext.at[lax.rem(p + 9, 12)], m_send.at[q], m_recv.at[q],
            device_id=(nbr(q), col), device_id_type=MESH)

    def m_arrival(q):
        e = landed(q)
        return pltpu.make_async_remote_copy(
            mext.at[e], mext.at[e], m_send.at[q], m_recv.at[q],
            device_id=(nbr(q), col), device_id_type=MESH)

    def s_rows(q, to_right):
        size = band + 1 + 2 * (q % 3)
        return pl.ds(pl.multiple_of(to_right * ((2 * band - size) * w), 8), size * w)

    def s_copy(q):
        p = pair(q)
        rows = s_rows(q, faces_right(q))
        return pltpu.make_async_remote_copy(
            sx.at[3 + p, rows], sx.at[lax.rem(p + 9, 12), rows], s_send.at[q], s_recv.at[q],
            device_id=(nbr(q), col), device_id_type=MESH)

    def s_arrival(q):
        e = landed(q)
        rows = s_rows(q, 1 - faces_right(q))
        return pltpu.make_async_remote_copy(
            sx.at[e, rows], sx.at[e, rows], s_send.at[q], s_recv.at[q],
            device_id=(nbr(q), col), device_id_type=MESH)

    def p_copy(q, i, who):
        return pltpu.make_async_remote_copy(
            panels[q].at[who], panels[q].at[who], p_send.at[i, q], p_recv.at[i, q],
            device_id=(row, peers[i]), device_id_type=MESH)

    def f_copy(q, i, who):
        return pltpu.make_async_remote_copy(
            panels[q].at[who, i], panels[q].at[who, i], f_send.at[i, q], f_recv.at[i, q],
            device_id=(row, peers[1 - i]), device_id_type=MESH)

    def p_start(q):
        for i in range(len(peers)):
            p_copy(q, i, col).start()

    def p_wait(q):
        for i in range(len(peers)):
            who = peers[i] if grid2 else lax.rem(col + n_col - 1 - i, n_col)
            p_copy(q, i, who).wait_recv()
        if grid2:
            for i in range(2):
                f_copy(q, i, peers[i]).start()

    for q in (0, 1):
        m_copy(2 - q).start()
        p_start(q)
    for q in (0, 5, 4, 3):
        m_copy(q).start()

    def build_left(e):
        x = mext[e]
        gap = jnp.zeros((w, nb), jnp.float32)
        first = jnp.concatenate([x[0].reshape(band * w, nb), gap], axis=0)
        second = jnp.concatenate([gap, x[1].reshape(band * w, nb)], axis=0)
        for i, part in enumerate((first, second)):
            hi, lo = split(part)
            lhi[e, :, i * nb:(i + 1) * nb] = hi
            llo[e, :, i * nb:(i + 1) * nb] = lo

    @pl.loop(0, 6)
    def _(i):
        build_left(3 + i)

    def build_right(q):
        p = pair(q)

        @pl.loop(0, steps)
        def _(m):
            for dj in range(2):
                for dr in range(2):
                    r = 2 * p + dr
                    s = 2 * m + dj - dr
                    t = rank[r, s + 1]
                    on = pat_wide(r, s)
                    x = panels[q][:, dr, t].reshape(nb, nb) * on
                    hi, lo = split(x)
                    at = (p * steps + m, pl.ds(dj * nb, nb), pl.ds(dr * nb, nb))
                    rhi[at] = hi
                    rlo[at] = lo

    def pat_wide(r, s):
        return rank[r, s + 1 + band + 2].astype(jnp.float32)

    def split_square(e, rows):
        hi, lo = split(sx[e, rows])
        shi[e, rows] = hi
        slo[e, rows] = lo

    def compute(q):
        p = pair(q)
        if grid2:
            for i in range(2):
                f_copy(q, i, 3 - col).wait_recv()
        near = 2 - q if q < 3 else 8 - q
        m_arrival(near).wait_recv()
        build_left(landed(near))
        build_right(q)
        sx[3 + p] = jnp.zeros((2 * band * w, wide), jnp.float32)

        @pl.loop(0, steps)
        def _(m):
            rows = pl.ds(pl.multiple_of(2 * m * w, 8), tall)
            k = p * steps + m
            sx[3 + p, rows] += dot3(lhi[p + m], llo[p + m], rhi[k], rlo[k])

        s_copy(q).start()
        split_square(3 + p, slice(None))

    for q in range(6):
        p_wait(q)
        if q + 2 < 6:
            p_start(q + 2)
        if q >= 1:
            compute(q - 1)
    compute(5)

    def cube(q):
        p = pair(q)
        acc[...] = jnp.zeros_like(acc)

        @pl.loop(0, steps)
        def _(m):
            rows = pl.ds(pl.multiple_of((2 * half - 2 * m) * w, 16), tall)
            e = p + m
            k = p * steps + m
            acc[...] += dot3(shi[e, rows], slo[e, rows], rhi[k], rlo[k])

        for dr in range(2):
            r = 2 * p + dr
            for i in range(band):
                lanes = pl.ds(dr * nb, nb)
                core = sx[3 + p, pl.ds((half + dr + i) * w, w), lanes]
                third = acc[pl.ds((dr + i) * w, w), lanes]
                out[r, i] = (3.0 * core - 2.0 * third) * pat[r, i].astype(jnp.float32)

    for group in ((3, 4, 5), (0, 1, 2)):
        for q in group:
            s_arrival(q).wait_recv()
            split_square(landed(q), s_rows(q, 1 - faces_right(q)))
        for q in group:
            cube(q)

    for q in range(6):
        m_copy(q).wait_send()
        s_copy(q).wait_send()
        for i in range(len(peers)):
            p_copy(q, i, col).wait_send()
        if grid2:
            for i in range(2):
                f_copy(q, i, peers[i]).wait_send()


def shards(n_row, n_col, density, pattern):
    rows, band, w, nb = density.shape
    half = (band - 1) // 2
    steps = half + 1
    slot = jnp.arange(band, dtype=jnp.int32)
    upto = jnp.sum(jnp.where(slot[None, None, :] <= slot[None, :, None], pattern[:, None, :], 0), axis=2)
    slots = jnp.sum((upto[:, None, :] <= jnp.arange(NZ, dtype=jnp.int32)[None, :, None]).astype(jnp.int32), axis=2)
    slots = jnp.clip(slots, 0, band - 1)
    rank = jnp.pad(jnp.clip(upto - 1, 0, NZ - 1), ((0, 0), (1, 1)))
    rank = jnp.concatenate([rank, jnp.pad(pattern, ((0, 0), (1, 1)))], axis=1)
    peers = 2 if n_col == 4 else n_col - 1
    tall, wide = (band + 1) * w, 2 * nb
    vmem, smem = pl.BlockSpec(memory_space=pltpu.VMEM), pl.BlockSpec(memory_space=pltpu.SMEM)
    f32, bf16, dma = jnp.float32, jnp.bfloat16, pltpu.SemaphoreType.DMA
    scratch = [pltpu.VMEM((n_col, 2, NZ, w, nb), f32) for _ in range(6)] + [
        pltpu.VMEM((12, 2, band, w, nb), f32),
        pltpu.VMEM((12, tall, wide), bf16),
        pltpu.VMEM((12, tall, wide), bf16),
        pltpu.VMEM((6 * steps, wide, wide), bf16),
        pltpu.VMEM((6 * steps, wide, wide), bf16),
        pltpu.VMEM((12, 2 * band * w, wide), f32),
        pltpu.VMEM((12, 2 * band * w, wide), bf16),
        pltpu.VMEM((12, 2 * band * w, wide), bf16),
        pltpu.VMEM((tall, wide), f32),
        dma((6,)), dma((6,)), dma((6,)), dma((6,)),
        dma((peers, 6)), dma((peers, 6)), dma((2, 6)), dma((2, 6)),
    ]
    return pl.pallas_call(
        functools.partial(kernel, n_row, n_col),
        out_shape=jax.ShapeDtypeStruct(density.shape, f32),
        in_specs=[vmem, smem, smem, smem],
        out_specs=vmem,
        scratch_shapes=scratch,
        compiler_params=pltpu.CompilerParams(
            collective_id=0, has_side_effects=True, vmem_limit_bytes=60 * 2**20),
        name="purify",
    )(density, pattern, rank, slots)


def solution(mesh):
    placed = (P("row", None, "col", None), P("row", None))
    body = functools.partial(shards, mesh.shape["row"], mesh.shape["col"])
    return jax.shard_map(
        body, mesh=mesh, in_specs=placed, out_specs=P("row", None, "col", None), check_vma=False
    )
```

```python
import functools

import jax
import jax.numpy as jnp
from jax import lax
from jax.experimental import pallas as pl
from jax.experimental.pallas import tpu as pltpu
from jax.sharding import PartitionSpec as P

NZ = 7
MESH = pl.DeviceIdType.MESH


def split(x):
    hi = x.astype(jnp.bfloat16)
    return hi, (x - hi.astype(jnp.float32)).astype(jnp.bfloat16)


def dot3(lhi, llo, rhi, rlo):
    f = functools.partial(jnp.dot, preferred_element_type=jnp.float32)
    return f(lhi, rhi) + f(lhi, rlo) + f(llo, rhi)


def kernel(n_row, n_col, d_ref, pat, out, *scratch):
    panels = scratch[:6]
    (mext, lhi, llo, rhi, rlo, sx, shi, slo, acc, rank, slots, m_send, m_recv, s_send,
     s_recv, p_send, p_recv, f_send, f_recv) = scratch[6:]
    w = d_ref.shape[2]
    band = d_ref.shape[1]
    half = (band - 1) // 2
    steps = half + 1
    nb = d_ref.shape[3]
    wide = 2 * nb
    tall = (band + 1) * w
    row = lax.axis_index("row")
    col = lax.axis_index("col")
    odd = lax.rem(row, 2)
    left = lax.rem(row + n_row - 1, n_row)
    right = lax.rem(row + 1, n_row)
    outer = left + odd * (right - left)
    mate = row + 1 - 2 * odd
    grid2 = n_col == 4
    if grid2:
        xn = col + 1 - 2 * lax.rem(col, 2)
        yn = lax.rem(col + 2, 4)
        peers = [xn, yn]
    else:
        peers = [lax.rem(col + d, n_col) for d in range(1, n_col)]

    def placed(v):
        return v + odd * (5 - 2 * v)

    def pair(q):
        return placed(2 - q if q < 3 else q)

    def faces_right(q):
        return odd if q < 3 else 1 - odd

    def nbr(q):
        return outer if q < 3 else mate

    def landed(q):
        p = 5 - pair(q)
        return lax.rem(p + 9, 12)

    barrier = pltpu.get_barrier_semaphore()
    for peer in peers:
        pl.semaphore_signal(barrier, inc=1, device_id=(row, peer), device_id_type=MESH)
    for peer in (left, right):
        pl.semaphore_signal(barrier, inc=1, device_id=(peer, col), device_id_type=MESH)

    @pl.loop(0, d_ref.shape[0])
    def _(r):
        count = jnp.int32(0)
        upto = []
        for edge in (0, band + 1):
            rank[r, edge] = jnp.int32(0)
            rank[r, 16 + edge] = jnp.int32(0)
        for s in range(band):
            on = pat[r, s]
            rank[r, s + 1] = jnp.minimum(count, NZ - 1)
            rank[r, 16 + s + 1] = on
            count = count + on
            upto.append(count)
        for t in range(NZ):
            place = jnp.int32(0)
            for s in range(band):
                place = place + jnp.where(upto[s] <= t, 1, 0)
            slots[r, t] = jnp.minimum(place, band - 1)

    for q in range(6):
        p = pair(q)
        for dr in range(2):
            r = 2 * p + dr
            for s in range(band):
                mext[3 + p, dr, pl.ds(NZ * w + s, 1)] = jnp.full(
                    (1, nb), pat[r, s].astype(jnp.float32))
            mext[3 + p, dr, pl.ds(NZ * w + band, 16 - band)] = jnp.zeros((16 - band, nb), jnp.float32)
            for t in range(NZ):
                x = d_ref[r, slots[r, t]]
                panels[q][col, dr, t] = x
                mext[3 + p, dr, pl.ds(t * w, w)] = x

    pl.semaphore_wait(barrier, len(peers) + 2)

    def m_copy(q):
        p = pair(q)
        return pltpu.make_async_remote_copy(
            mext.at[3 + p], mext.at[lax.rem(p + 9, 12)], m_send.at[q], m_recv.at[q],
            device_id=(nbr(q), col), device_id_type=MESH)

    def m_arrival(q):
        e = landed(q)
        return pltpu.make_async_remote_copy(
            mext.at[e], mext.at[e], m_send.at[q], m_recv.at[q],
            device_id=(nbr(q), col), device_id_type=MESH)

    def s_rows(q, to_right):
        size = band + 1 + 2 * (q % 3)
        return pl.ds(pl.multiple_of(to_right * ((2 * band - size) * w), 8), size * w)

    def s_copy(q):
        p = pair(q)
        rows = s_rows(q, faces_right(q))
        return pltpu.make_async_remote_copy(
            sx.at[3 + p, rows], sx.at[lax.rem(p + 9, 12), rows], s_send.at[q], s_recv.at[q],
            device_id=(nbr(q), col), device_id_type=MESH)

    def s_arrival(q):
        e = landed(q)
        rows = s_rows(q, 1 - faces_right(q))
        return pltpu.make_async_remote_copy(
            sx.at[e, rows], sx.at[e, rows], s_send.at[q], s_recv.at[q],
            device_id=(nbr(q), col), device_id_type=MESH)

    def p_copy(q, i, who):
        return pltpu.make_async_remote_copy(
            panels[q].at[who], panels[q].at[who], p_send.at[i, q], p_recv.at[i, q],
            device_id=(row, peers[i]), device_id_type=MESH)

    def f_copy(q, i, who):
        return pltpu.make_async_remote_copy(
            panels[q].at[who, i], panels[q].at[who, i], f_send.at[i, q], f_recv.at[i, q],
            device_id=(row, peers[1 - i]), device_id_type=MESH)

    def p_start(q):
        for i in range(len(peers)):
            p_copy(q, i, col).start()

    def p_wait(q):
        for i in range(len(peers)):
            who = peers[i] if grid2 else lax.rem(col + n_col - 1 - i, n_col)
            p_copy(q, i, who).wait_recv()
        if grid2:
            for i in range(2):
                f_copy(q, i, peers[i]).start()

    for q in (0, 1):
        m_copy(2 - q).start()
        p_start(q)
    for q in (0, 5, 4, 3):
        m_copy(q).start()

    def store_left(e, blocks):
        gap = jnp.zeros((w, nb), jnp.float32)
        first = jnp.concatenate(blocks[0] + [gap], axis=0)
        second = jnp.concatenate([gap] + blocks[1], axis=0)
        for i, part in enumerate((first, second)):
            hi, lo = split(part)
            lhi[e, :, i * nb:(i + 1) * nb] = hi
            llo[e, :, i * nb:(i + 1) * nb] = lo

    def build_own(p):
        blocks = []
        for dr in range(2):
            r = 2 * p + dr
            blocks.append([d_ref[r, s] * pat[r, s].astype(jnp.float32) for s in range(band)])
        store_left(3 + p, blocks)

    def build_left(e):
        blocks = []
        for dr in range(2):
            here = [jnp.ones((1, nb), jnp.float32)]
            row_blocks = []
            for s in range(band):
                on = mext[e, dr, pl.ds(NZ * w + s, 1)]
                total = jnp.zeros((w, nb), jnp.float32)
                for t in range(max(0, s - band + NZ), min(NZ, s + 1)):
                    total = total + (here[t] * on) * mext[e, dr, pl.ds(t * w, w)]
                row_blocks.append(total)
                stay = [h * (1.0 - on) for h in here] + [jnp.zeros((1, nb), jnp.float32)]
                move = [jnp.zeros((1, nb), jnp.float32)] + [h * on for h in here]
                here = [a + b for a, b in zip(stay, move)][:NZ]
            blocks.append(row_blocks)
        store_left(e, blocks)

    @pl.loop(0, 6)
    def _(i):
        build_own(i)

    def build_right(q):
        p = pair(q)

        @pl.loop(0, steps)
        def _(m):
            for dj in range(2):
                for dr in range(2):
                    r = 2 * p + dr
                    s = 2 * m + dj - dr
                    t = rank[r, s + 1]
                    on = pat_wide(r, s)
                    x = panels[q][:, dr, t].reshape(nb, nb) * on
                    hi, lo = split(x)
                    at = (p * steps + m, pl.ds(dj * nb, nb), pl.ds(dr * nb, nb))
                    rhi[at] = hi
                    rlo[at] = lo

    def pat_wide(r, s):
        return rank[r, s + 1 + 16].astype(jnp.float32)

    def split_square(e, rows):
        hi, lo = split(sx[e, rows])
        shi[e, rows] = hi
        slo[e, rows] = lo

    def compute(q):
        p = pair(q)
        if grid2:
            for i in range(2):
                f_copy(q, i, 3 - col).wait_recv()
        near = 2 - q if q < 3 else 8 - q
        m_arrival(near).wait_recv()
        build_left(landed(near))
        build_right(q)
        sx[3 + p] = jnp.zeros((2 * band * w, wide), jnp.float32)

        @pl.loop(0, steps)
        def _(m):
            rows = pl.ds(pl.multiple_of(2 * m * w, 8), tall)
            k = p * steps + m
            sx[3 + p, rows] += dot3(lhi[p + m], llo[p + m], rhi[k], rlo[k])

        s_copy(q).start()
        split_square(3 + p, slice(None))
        own = 2 - q if q < 3 else q
        low, high = (own, 2) if q < 3 else (own - 3, own)

        @pl.loop(low, high + 1)
        def _(v):
            add_third(p, 3 + placed(v))

        if high > low:
            @pl.loop(low + 1 if q < 3 else low, high + 1 if q < 3 else high)
            def _(v):
                add_third(placed(v), 3 + p)

    def add_third(p, e):
        m = e - p
        rows = pl.ds(pl.multiple_of((2 * half - 2 * m) * w, 16), tall)
        k = p * steps + m
        acc[p] += dot3(shi[e, rows], slo[e, rows], rhi[k], rlo[k])

    def add_halo(q):
        s_arrival(q).wait_recv()
        e = landed(q)
        split_square(e, s_rows(q, 1 - faces_right(q)))
        a = q % 3

        @pl.loop(0 if q < 3 else 5 - a, a + 1 if q < 3 else 6)
        def _(v):
            add_third(placed(v), e)

    acc[...] = jnp.zeros_like(acc)

    for q in range(6):
        p_wait(q)
        if q + 2 < 6:
            p_start(q + 2)
        if q >= 1:
            compute(q - 1)
    add_halo(0)
    add_halo(1)
    compute(5)

    def finish(q):
        p = pair(q)
        for dr in range(2):
            r = 2 * p + dr
            for i in range(band):
                lanes = pl.ds(dr * nb, nb)
                core = sx[3 + p, pl.ds((half + dr + i) * w, w), lanes]
                third = acc[p, pl.ds((dr + i) * w, w), lanes]
                out[r, i] = (3.0 * core - 2.0 * third) * pat[r, i].astype(jnp.float32)

    add_halo(2)
    for q in (0, 1, 2):
        finish(q)
    for q in (3, 4, 5):
        add_halo(q)
    for q in (3, 4, 5):
        finish(q)

    for q in range(6):
        m_copy(q).wait_send()
        s_copy(q).wait_send()
        for i in range(len(peers)):
            p_copy(q, i, col).wait_send()
        if grid2:
            for i in range(2):
                f_copy(q, i, peers[i]).wait_send()


def shards(n_row, n_col, density, pattern):
    rows, band, w, nb = density.shape
    steps = (band + 1) // 2
    peers = 2 if n_col == 4 else n_col - 1
    tall, wide = (band + 1) * w, 2 * nb
    vmem, smem = pl.BlockSpec(memory_space=pltpu.VMEM), pl.BlockSpec(memory_space=pltpu.SMEM)
    f32, bf16, dma = jnp.float32, jnp.bfloat16, pltpu.SemaphoreType.DMA
    scratch = [pltpu.VMEM((n_col, 2, NZ, w, nb), f32) for _ in range(6)] + [
        pltpu.VMEM((12, 2, NZ * w + 16, nb), f32),
        pltpu.VMEM((12, tall, wide), bf16),
        pltpu.VMEM((12, tall, wide), bf16),
        pltpu.VMEM((6 * steps, wide, wide), bf16),
        pltpu.VMEM((6 * steps, wide, wide), bf16),
        pltpu.VMEM((12, 2 * band * w, wide), f32),
        pltpu.VMEM((12, 2 * band * w, wide), bf16),
        pltpu.VMEM((12, 2 * band * w, wide), bf16),
        pltpu.VMEM((6, tall, wide), f32),
        pltpu.SMEM((rows, 32), jnp.int32),
        pltpu.SMEM((rows, 8), jnp.int32),
        dma((6,)), dma((6,)), dma((6,)), dma((6,)),
        dma((peers, 6)), dma((peers, 6)), dma((2, 6)), dma((2, 6)),
    ]
    return pl.pallas_call(
        functools.partial(kernel, n_row, n_col),
        out_shape=jax.ShapeDtypeStruct(density.shape, f32),
        in_specs=[vmem, smem],
        out_specs=vmem,
        scratch_shapes=scratch,
        compiler_params=pltpu.CompilerParams(
            collective_id=0, has_side_effects=True, vmem_limit_bytes=60 * 2**20),
        name="purify",
    )(density, pattern)


def solution(mesh):
    placed = (P("row", None, "col", None), P("row", None))
    body = functools.partial(shards, mesh.shape["row"], mesh.shape["col"])
    return jax.shard_map(
        body, mesh=mesh, in_specs=placed, out_specs=P("row", None, "col", None), check_vma=False
    )
```

```python
import functools

import jax
import jax.numpy as jnp
from jax import lax
from jax.experimental import pallas as pl
from jax.experimental.pallas import tpu as pltpu
from jax.sharding import PartitionSpec as P

NZ = 7
MESH = pl.DeviceIdType.MESH


def split(x):
    hi = x.astype(jnp.bfloat16)
    return hi, (x - hi.astype(jnp.float32)).astype(jnp.bfloat16)


def dot3(lhi, llo, rhi, rlo):
    left = jnp.concatenate([lhi, lhi, llo], axis=1)
    right = jnp.concatenate([rhi, rlo, rhi], axis=0)
    return jnp.dot(left, right, preferred_element_type=jnp.float32)


def kernel(n_row, n_col, d_hbm, pat, out, *scratch):
    panels = scratch[:6]
    (d_ref, d_sem, mext, lhi, llo, rhi, rlo, sx, shi, slo, acc, rank, slots, m_send, m_recv, s_send,
     s_recv, p_send, p_recv, f_send, f_recv) = scratch[6:]
    w = d_ref.shape[2]
    band = d_ref.shape[1]
    half = (band - 1) // 2
    steps = half + 1
    nb = d_ref.shape[3]
    wide = 2 * nb
    tall = (band + 1) * w
    row = lax.axis_index("row")
    col = lax.axis_index("col")
    odd = lax.rem(row, 2)
    left = lax.rem(row + n_row - 1, n_row)
    right = lax.rem(row + 1, n_row)
    outer = left + odd * (right - left)
    mate = row + 1 - 2 * odd
    grid2 = n_col == 4
    if grid2:
        xn = col + 1 - 2 * lax.rem(col, 2)
        yn = lax.rem(col + 2, 4)
        peers = [xn, yn]
    else:
        peers = [lax.rem(col + d, n_col) for d in range(1, n_col)]

    def placed(v):
        return v + odd * (5 - 2 * v)

    def pair(q):
        return placed(2 - q if q < 3 else q)

    def faces_right(q):
        return odd if q < 3 else 1 - odd

    def nbr(q):
        return outer if q < 3 else mate

    def landed(q):
        p = 5 - pair(q)
        return lax.rem(p + 9, 12)

    barrier = pltpu.get_barrier_semaphore()
    for peer in peers:
        pl.semaphore_signal(barrier, inc=1, device_id=(row, peer), device_id_type=MESH)
    for peer in (left, right):
        pl.semaphore_signal(barrier, inc=1, device_id=(peer, col), device_id_type=MESH)

    fetch = pltpu.make_async_copy(d_hbm, d_ref, d_sem)
    fetch.start()

    @pl.loop(0, d_ref.shape[0])
    def _(r):
        count = jnp.int32(0)
        upto = []
        for edge in (0, band + 1):
            rank[r, edge] = jnp.int32(0)
            rank[r, 16 + edge] = jnp.int32(0)
        for s in range(band):
            on = pat[r, s]
            rank[r, s + 1] = jnp.minimum(count, NZ - 1)
            rank[r, 16 + s + 1] = on
            count = count + on
            upto.append(count)
        for t in range(NZ):
            place = jnp.int32(0)
            for s in range(band):
                place = place + jnp.where(upto[s] <= t, 1, 0)
            slots[r, t] = jnp.minimum(place, band - 1)

    fetch.wait()
    pl.semaphore_wait(barrier, len(peers) + 2)

    def m_copy(q):
        p = pair(q)
        return pltpu.make_async_remote_copy(
            mext.at[3 + p], mext.at[lax.rem(p + 9, 12)], m_send.at[q], m_recv.at[q],
            device_id=(nbr(q), col), device_id_type=MESH)

    def m_arrival(q):
        e = landed(q)
        return pltpu.make_async_remote_copy(
            mext.at[e], mext.at[e], m_send.at[q], m_recv.at[q],
            device_id=(nbr(q), col), device_id_type=MESH)

    def s_rows(q, to_right):
        size = band + 1 + 2 * (q % 3)
        return pl.ds(pl.multiple_of(to_right * ((2 * band - size) * w), 8), size * w)

    def s_copy(q):
        p = pair(q)
        rows = s_rows(q, faces_right(q))
        return pltpu.make_async_remote_copy(
            sx.at[3 + p, rows], sx.at[lax.rem(p + 9, 12), rows], s_send.at[q], s_recv.at[q],
            device_id=(nbr(q), col), device_id_type=MESH)

    def s_arrival(q):
        e = landed(q)
        rows = s_rows(q, 1 - faces_right(q))
        return pltpu.make_async_remote_copy(
            sx.at[e, rows], sx.at[e, rows], s_send.at[q], s_recv.at[q],
            device_id=(nbr(q), col), device_id_type=MESH)

    def p_copy(q, i, who):
        return pltpu.make_async_remote_copy(
            panels[q].at[who], panels[q].at[who], p_send.at[i, q], p_recv.at[i, q],
            device_id=(row, peers[i]), device_id_type=MESH)

    def f_copy(q, i, who):
        return pltpu.make_async_remote_copy(
            panels[q].at[who, i], panels[q].at[who, i], f_send.at[i, q], f_recv.at[i, q],
            device_id=(row, peers[1 - i]), device_id_type=MESH)

    def p_start(q):
        for i in range(len(peers)):
            p_copy(q, i, col).start()

    def p_wait(q):
        for i in range(len(peers)):
            who = peers[i] if grid2 else lax.rem(col + n_col - 1 - i, n_col)
            p_copy(q, i, who).wait_recv()
        if grid2:
            for i in range(2):
                f_copy(q, i, peers[i]).start()

    def pack(q):
        p = pair(q)
        for dr in range(2):
            r = 2 * p + dr
            for s in range(band):
                mext[3 + p, dr, pl.ds(NZ * w + s, 1)] = jnp.full(
                    (1, nb), pat[r, s].astype(jnp.float32))
            mext[3 + p, dr, pl.ds(NZ * w + band, 16 - band)] = jnp.zeros((16 - band, nb), jnp.float32)
            for t in range(NZ):
                x = d_ref[r, slots[r, t]]
                panels[q][col, dr, t] = x
                mext[3 + p, dr, pl.ds(t * w, w)] = x

    for q in (0, 1):
        pack(q)
        p_start(q)
    pack(2)
    for q in (2, 1, 0):
        m_copy(q).start()
    for q in (5, 4, 3):
        pack(q)
        m_copy(q).start()

    def store_left(e, blocks):
        gap = jnp.zeros((w, nb), jnp.float32)
        first = jnp.concatenate(blocks[0] + [gap], axis=0)
        second = jnp.concatenate([gap] + blocks[1], axis=0)
        for i, part in enumerate((first, second)):
            hi, lo = split(part)
            lhi[e, :, i * nb:(i + 1) * nb] = hi
            llo[e, :, i * nb:(i + 1) * nb] = lo

    def build_own(p):
        blocks = []
        for dr in range(2):
            r = 2 * p + dr
            blocks.append([d_ref[r, s] * pat[r, s].astype(jnp.float32) for s in range(band)])
        store_left(3 + p, blocks)

    def build_left(e):
        blocks = []
        for dr in range(2):
            here = [jnp.ones((1, nb), jnp.float32)]
            row_blocks = []
            for s in range(band):
                on = mext[e, dr, pl.ds(NZ * w + s, 1)]
                total = jnp.zeros((w, nb), jnp.float32)
                for t in range(max(0, s - band + NZ), min(NZ, s + 1)):
                    total = total + (here[t] * on) * mext[e, dr, pl.ds(t * w, w)]
                row_blocks.append(total)
                stay = [h * (1.0 - on) for h in here] + [jnp.zeros((1, nb), jnp.float32)]
                move = [jnp.zeros((1, nb), jnp.float32)] + [h * on for h in here]
                here = [a + b for a, b in zip(stay, move)][:NZ]
            blocks.append(row_blocks)
        store_left(e, blocks)

    @pl.loop(0, 6)
    def _(i):
        build_own(i)

    def build_right(q):
        p = pair(q)

        @pl.loop(0, steps)
        def _(m):
            for dj in range(2):
                for dr in range(2):
                    r = 2 * p + dr
                    s = 2 * m + dj - dr
                    t = rank[r, s + 1]
                    on = pat_wide(r, s)
                    x = panels[q][:, dr, t].reshape(nb, nb) * on
                    hi, lo = split(x)
                    at = (p * steps + m, pl.ds(dj * nb, nb), pl.ds(dr * nb, nb))
                    rhi[at] = hi
                    rlo[at] = lo

    def pat_wide(r, s):
        return rank[r, s + 1 + 16].astype(jnp.float32)

    def split_square(e, rows):
        hi, lo = split(sx[e, rows])
        shi[e, rows] = hi
        slo[e, rows] = lo

    def compute(q):
        p = pair(q)
        if grid2:
            for i in range(2):
                f_copy(q, i, 3 - col).wait_recv()
        near = 2 - q if q < 3 else 8 - q
        m_arrival(near).wait_recv()
        build_left(landed(near))
        build_right(q)
        sx[3 + p] = jnp.zeros((2 * band * w, wide), jnp.float32)

        @pl.loop(0, steps)
        def _(m):
            rows = pl.ds(pl.multiple_of(2 * m * w, 8), tall)
            k = p * steps + m
            sx[3 + p, rows] += dot3(lhi[p + m], llo[p + m], rhi[k], rlo[k])

        s_copy(q).start()
        split_square(3 + p, slice(None))
        own = 2 - q if q < 3 else q
        low, high = (own, 2) if q < 3 else (own - 3, own)

        @pl.loop(low, high + 1)
        def _(v):
            add_third(p, 3 + placed(v))

        if high > low:
            @pl.loop(low + 1 if q < 3 else low, high + 1 if q < 3 else high)
            def _(v):
                add_third(placed(v), 3 + p)

    def add_third(p, e):
        m = e - p
        rows = pl.ds(pl.multiple_of((2 * half - 2 * m) * w, 16), tall)
        k = p * steps + m
        acc[p] += dot3(shi[e, rows], slo[e, rows], rhi[k], rlo[k])

    def add_halo(q):
        s_arrival(q).wait_recv()
        e = landed(q)
        split_square(e, s_rows(q, 1 - faces_right(q)))
        a = q % 3

        @pl.loop(0 if q < 3 else 5 - a, a + 1 if q < 3 else 6)
        def _(v):
            add_third(placed(v), e)

    acc[...] = jnp.zeros_like(acc)

    for q in range(6):
        p_wait(q)
        if q + 2 < 6:
            p_start(q + 2)
        if q >= 1:
            compute(q - 1)
    add_halo(0)
    add_halo(1)
    compute(5)

    def finish(q):
        p = pair(q)
        for dr in range(2):
            r = 2 * p + dr
            for i in range(band):
                lanes = pl.ds(dr * nb, nb)
                core = sx[3 + p, pl.ds((half + dr + i) * w, w), lanes]
                third = acc[p, pl.ds((dr + i) * w, w), lanes]
                out[r, i] = (3.0 * core - 2.0 * third) * pat[r, i].astype(jnp.float32)

    add_halo(2)
    for q in (0, 1, 2):
        finish(q)
    for q in (3, 4, 5):
        add_halo(q)
    for q in (3, 4, 5):
        finish(q)

    for q in range(6):
        m_copy(q).wait_send()
        s_copy(q).wait_send()
        for i in range(len(peers)):
            p_copy(q, i, col).wait_send()
        if grid2:
            for i in range(2):
                f_copy(q, i, peers[i]).wait_send()


def shards(n_row, n_col, density, pattern):
    rows, band, w, nb = density.shape
    steps = (band + 1) // 2
    peers = 2 if n_col == 4 else n_col - 1
    tall, wide = (band + 1) * w, 2 * nb
    vmem, smem = pl.BlockSpec(memory_space=pltpu.VMEM), pl.BlockSpec(memory_space=pltpu.SMEM)
    f32, bf16, dma = jnp.float32, jnp.bfloat16, pltpu.SemaphoreType.DMA
    scratch = [pltpu.VMEM((n_col, 2, NZ, w, nb), f32) for _ in range(6)] + [
        pltpu.VMEM(density.shape, f32),
        dma,
        pltpu.VMEM((12, 2, NZ * w + 16, nb), f32),
        pltpu.VMEM((12, tall, wide), bf16),
        pltpu.VMEM((12, tall, wide), bf16),
        pltpu.VMEM((6 * steps, wide, wide), bf16),
        pltpu.VMEM((6 * steps, wide, wide), bf16),
        pltpu.VMEM((12, 2 * band * w, wide), f32),
        pltpu.VMEM((12, 2 * band * w, wide), bf16),
        pltpu.VMEM((12, 2 * band * w, wide), bf16),
        pltpu.VMEM((6, tall, wide), f32),
        pltpu.SMEM((rows, 32), jnp.int32),
        pltpu.SMEM((rows, 8), jnp.int32),
        dma((6,)), dma((6,)), dma((6,)), dma((6,)),
        dma((peers, 6)), dma((peers, 6)), dma((2, 6)), dma((2, 6)),
    ]
    return pl.pallas_call(
        functools.partial(kernel, n_row, n_col),
        out_shape=pltpu.VMEM(density.shape, f32),
        in_specs=[pl.BlockSpec(memory_space=pl.ANY), smem],
        out_specs=vmem,
        scratch_shapes=scratch,
        compiler_params=pltpu.CompilerParams(
            collective_id=0, has_side_effects=True, vmem_limit_bytes=60 * 2**20),
        name="purify",
    )(density, pattern)


def solution(mesh):
    placed = (P("row", None, "col", None), P("row", None))
    body = functools.partial(shards, mesh.shape["row"], mesh.shape["col"])
    return jax.shard_map(
        body, mesh=mesh, in_specs=placed, out_specs=P("row", None, "col", None), check_vma=False
    )
```

```python
import functools

import jax
import jax.numpy as jnp
from jax import lax
from jax.experimental import pallas as pl
from jax.experimental.pallas import tpu as pltpu
from jax.sharding import PartitionSpec as P

NZ = 7
MESH = pl.DeviceIdType.MESH


def split(x):
    hi = x.astype(jnp.bfloat16)
    return hi, (x - hi.astype(jnp.float32)).astype(jnp.bfloat16)


def dot3(lhi, llo, rhi, rlo):
    left = jnp.concatenate([lhi, lhi, llo], axis=1)
    right = jnp.concatenate([rhi, rlo, rhi], axis=0)
    return jnp.dot(left, right, preferred_element_type=jnp.float32)


def kernel(n_row, n_col, d_hbm, pat, out, *scratch):
    panels = scratch[:6]
    (d_ref, d_sem, mext, lhi, llo, rhi, rlo, sx, shi, slo, acc, rank, slots, m_send, m_recv, s_send,
     s_recv, p_send, p_recv, f_send, f_recv) = scratch[6:]
    w = d_ref.shape[2]
    band = d_ref.shape[1]
    half = (band - 1) // 2
    steps = half + 1
    nb = d_ref.shape[3]
    wide = 2 * nb
    tall = (band + 1) * w
    row = lax.axis_index("row")
    col = lax.axis_index("col")
    odd = lax.rem(row, 2)
    left = lax.rem(row + n_row - 1, n_row)
    right = lax.rem(row + 1, n_row)
    outer = left + odd * (right - left)
    mate = row + 1 - 2 * odd
    grid2 = n_col == 4
    if grid2:
        xn = col + 1 - 2 * lax.rem(col, 2)
        yn = lax.rem(col + 2, 4)
        peers = [xn, yn]
    else:
        peers = [lax.rem(col + d, n_col) for d in range(1, n_col)]

    def placed(v):
        return v + odd * (5 - 2 * v)

    def pair(q):
        return placed(2 - q if q < 3 else q)

    def faces_right(q):
        return odd if q < 3 else 1 - odd

    def nbr(q):
        return outer if q < 3 else mate

    def landed(q):
        p = 5 - pair(q)
        return lax.rem(p + 9, 12)

    barrier = pltpu.get_barrier_semaphore()
    for peer in peers:
        pl.semaphore_signal(barrier, inc=1, device_id=(row, peer), device_id_type=MESH)
    for peer in (left, right):
        pl.semaphore_signal(barrier, inc=1, device_id=(peer, col), device_id_type=MESH)

    fetch = pltpu.make_async_copy(d_hbm, d_ref, d_sem)
    fetch.start()

    @pl.loop(0, d_ref.shape[0])
    def _(r):
        count = jnp.int32(0)
        upto = []
        for edge in (0, band + 1):
            rank[r, edge] = jnp.int32(0)
            rank[r, 16 + edge] = jnp.int32(0)
        for s in range(band):
            on = pat[r, s]
            rank[r, s + 1] = jnp.minimum(count, NZ - 1)
            rank[r, 16 + s + 1] = on
            count = count + on
            upto.append(count)
        for t in range(NZ):
            place = jnp.int32(0)
            for s in range(band):
                place = place + jnp.where(upto[s] <= t, 1, 0)
            slots[r, t] = jnp.minimum(place, band - 1)

    fetch.wait()
    pl.semaphore_wait(barrier, len(peers) + 2)

    def m_copy(q):
        p = pair(q)
        return pltpu.make_async_remote_copy(
            mext.at[3 + p], mext.at[lax.rem(p + 9, 12)], m_send.at[q], m_recv.at[q],
            device_id=(nbr(q), col), device_id_type=MESH)

    def m_arrival(q):
        e = landed(q)
        return pltpu.make_async_remote_copy(
            mext.at[e], mext.at[e], m_send.at[q], m_recv.at[q],
            device_id=(nbr(q), col), device_id_type=MESH)

    def s_rows(q, to_right):
        size = band + 1 + 2 * (q % 3)
        return pl.ds(pl.multiple_of(to_right * ((2 * band - size) * w), 8), size * w)

    def s_copy(q):
        p = pair(q)
        rows = s_rows(q, faces_right(q))
        return pltpu.make_async_remote_copy(
            sx.at[3 + p, rows], sx.at[lax.rem(p + 9, 12), rows], s_send.at[q], s_recv.at[q],
            device_id=(nbr(q), col), device_id_type=MESH)

    def s_arrival(q):
        e = landed(q)
        rows = s_rows(q, 1 - faces_right(q))
        return pltpu.make_async_remote_copy(
            sx.at[e, rows], sx.at[e, rows], s_send.at[q], s_recv.at[q],
            device_id=(nbr(q), col), device_id_type=MESH)

    def p_copy(q, i, who, part):
        at = panels[q].at[who, (i + part) % 2]
        return pltpu.make_async_remote_copy(
            at, at, p_send.at[i, part, q], p_recv.at[i, part, q],
            device_id=(row, peers[i]), device_id_type=MESH)

    def f_copy(q, i, who):
        return pltpu.make_async_remote_copy(
            panels[q].at[who, i], panels[q].at[who, i], f_send.at[i, q], f_recv.at[i, q],
            device_id=(row, peers[1 - i]), device_id_type=MESH)

    def p_start(q):
        for part in range(2):
            for i in range(len(peers)):
                p_copy(q, i, col, part).start()

    def p_wait(q, part):
        for i in range(len(peers)):
            who = peers[i] if grid2 else lax.rem(col + n_col - 1 - i, n_col)
            p_copy(q, i, who, part).wait_recv()
            if grid2 and part == 0:
                f_copy(q, i, who).start()

    def pack(q):
        p = pair(q)
        for dr in range(2):
            r = 2 * p + dr
            for s in range(band):
                mext[3 + p, dr, pl.ds(NZ * w + s, 1)] = jnp.full(
                    (1, nb), pat[r, s].astype(jnp.float32))
            mext[3 + p, dr, pl.ds(NZ * w + band, 16 - band)] = jnp.zeros((16 - band, nb), jnp.float32)
            for t in range(NZ):
                x = d_ref[r, slots[r, t]]
                panels[q][col, dr, t] = x
                mext[3 + p, dr, pl.ds(t * w, w)] = x

    for q in (0, 1):
        pack(q)
        p_start(q)
    pack(2)
    for q in (2, 1, 0):
        m_copy(q).start()
    for q in (5, 4, 3):
        pack(q)
        m_copy(q).start()

    def store_left(e, blocks):
        gap = jnp.zeros((w, nb), jnp.float32)
        first = jnp.concatenate(blocks[0] + [gap], axis=0)
        second = jnp.concatenate([gap] + blocks[1], axis=0)
        for i, part in enumerate((first, second)):
            hi, lo = split(part)
            lhi[e, :, i * nb:(i + 1) * nb] = hi
            llo[e, :, i * nb:(i + 1) * nb] = lo

    def build_own(p):
        blocks = []
        for dr in range(2):
            r = 2 * p + dr
            blocks.append([d_ref[r, s] * pat[r, s].astype(jnp.float32) for s in range(band)])
        store_left(3 + p, blocks)

    def build_left(e):
        blocks = []
        for dr in range(2):
            here = [jnp.ones((1, nb), jnp.float32)]
            row_blocks = []
            for s in range(band):
                on = mext[e, dr, pl.ds(NZ * w + s, 1)]
                total = jnp.zeros((w, nb), jnp.float32)
                for t in range(max(0, s - band + NZ), min(NZ, s + 1)):
                    total = total + (here[t] * on) * mext[e, dr, pl.ds(t * w, w)]
                row_blocks.append(total)
                stay = [h * (1.0 - on) for h in here] + [jnp.zeros((1, nb), jnp.float32)]
                move = [jnp.zeros((1, nb), jnp.float32)] + [h * on for h in here]
                here = [a + b for a, b in zip(stay, move)][:NZ]
            blocks.append(row_blocks)
        store_left(e, blocks)

    @pl.loop(0, 6)
    def _(i):
        build_own(i)

    def build_right(q):
        p = pair(q)

        @pl.loop(0, steps)
        def _(m):
            for dj in range(2):
                for dr in range(2):
                    r = 2 * p + dr
                    s = 2 * m + dj - dr
                    t = rank[r, s + 1]
                    on = pat_wide(r, s)
                    x = panels[q][:, dr, t].reshape(nb, nb) * on
                    hi, lo = split(x)
                    at = (p * steps + m, pl.ds(dj * nb, nb), pl.ds(dr * nb, nb))
                    rhi[at] = hi
                    rlo[at] = lo

    def pat_wide(r, s):
        return rank[r, s + 1 + 16].astype(jnp.float32)

    def split_square(e, rows):
        hi, lo = split(sx[e, rows])
        shi[e, rows] = hi
        slo[e, rows] = lo

    def compute(q):
        p = pair(q)
        p_wait(q, 1)
        if grid2:
            for i in range(2):
                f_copy(q, i, 3 - col).wait_recv()
        near = 2 - q if q < 3 else 8 - q
        m_arrival(near).wait_recv()
        build_left(landed(near))
        build_right(q)
        sx[3 + p] = jnp.zeros((2 * band * w, wide), jnp.float32)

        @pl.loop(0, steps)
        def _(m):
            rows = pl.ds(pl.multiple_of(2 * m * w, 8), tall)
            k = p * steps + m
            sx[3 + p, rows] += dot3(lhi[p + m], llo[p + m], rhi[k], rlo[k])

        s_copy(q).start()
        split_square(3 + p, slice(None))
        own = 2 - q if q < 3 else q
        low, high = (own, 2) if q < 3 else (own - 3, own)

        @pl.loop(low, high + 1)
        def _(v):
            add_third(p, 3 + placed(v))

        if high > low:
            @pl.loop(low + 1 if q < 3 else low, high + 1 if q < 3 else high)
            def _(v):
                add_third(placed(v), 3 + p)

    def add_third(p, e):
        m = e - p
        rows = pl.ds(pl.multiple_of((2 * half - 2 * m) * w, 16), tall)
        k = p * steps + m
        acc[p] += dot3(shi[e, rows], slo[e, rows], rhi[k], rlo[k])

    def add_halo(q):
        s_arrival(q).wait_recv()
        e = landed(q)
        split_square(e, s_rows(q, 1 - faces_right(q)))
        a = q % 3

        @pl.loop(0 if q < 3 else 5 - a, a + 1 if q < 3 else 6)
        def _(v):
            add_third(placed(v), e)

    acc[...] = jnp.zeros_like(acc)

    for q in range(6):
        p_wait(q, 0)
        if q + 2 < 6:
            p_start(q + 2)
        if q >= 1:
            compute(q - 1)
    add_halo(0)
    add_halo(1)
    compute(5)

    def finish(q):
        p = pair(q)
        for dr in range(2):
            r = 2 * p + dr
            for i in range(band):
                lanes = pl.ds(dr * nb, nb)
                core = sx[3 + p, pl.ds((half + dr + i) * w, w), lanes]
                third = acc[p, pl.ds((dr + i) * w, w), lanes]
                out[r, i] = (3.0 * core - 2.0 * third) * pat[r, i].astype(jnp.float32)

    add_halo(2)
    for q in (0, 1, 2):
        finish(q)
    for q in (3, 4, 5):
        add_halo(q)
    for q in (3, 4, 5):
        finish(q)

    for q in range(6):
        m_copy(q).wait_send()
        s_copy(q).wait_send()
        for i in range(len(peers)):
            for part in range(2):
                p_copy(q, i, col, part).wait_send()
        if grid2:
            for i in range(2):
                f_copy(q, i, peers[i]).wait_send()


def shards(n_row, n_col, density, pattern):
    rows, band, w, nb = density.shape
    steps = (band + 1) // 2
    peers = 2 if n_col == 4 else n_col - 1
    tall, wide = (band + 1) * w, 2 * nb
    vmem, smem = pl.BlockSpec(memory_space=pltpu.VMEM), pl.BlockSpec(memory_space=pltpu.SMEM)
    f32, bf16, dma = jnp.float32, jnp.bfloat16, pltpu.SemaphoreType.DMA
    scratch = [pltpu.VMEM((n_col, 2, NZ, w, nb), f32) for _ in range(6)] + [
        pltpu.VMEM(density.shape, f32),
        dma,
        pltpu.VMEM((12, 2, NZ * w + 16, nb), f32),
        pltpu.VMEM((12, tall, wide), bf16),
        pltpu.VMEM((12, tall, wide), bf16),
        pltpu.VMEM((6 * steps, wide, wide), bf16),
        pltpu.VMEM((6 * steps, wide, wide), bf16),
        pltpu.VMEM((12, 2 * band * w, wide), f32),
        pltpu.VMEM((12, 2 * band * w, wide), bf16),
        pltpu.VMEM((12, 2 * band * w, wide), bf16),
        pltpu.VMEM((6, tall, wide), f32),
        pltpu.SMEM((rows, 32), jnp.int32),
        pltpu.SMEM((rows, 8), jnp.int32),
        dma((6,)), dma((6,)), dma((6,)), dma((6,)),
        dma((peers, 2, 6)), dma((peers, 2, 6)), dma((2, 6)), dma((2, 6)),
    ]
    return pl.pallas_call(
        functools.partial(kernel, n_row, n_col),
        out_shape=pltpu.VMEM(density.shape, f32),
        in_specs=[pl.BlockSpec(memory_space=pl.ANY), smem],
        out_specs=vmem,
        scratch_shapes=scratch,
        compiler_params=pltpu.CompilerParams(
            collective_id=0, has_side_effects=True, vmem_limit_bytes=60 * 2**20),
        name="purify",
    )(density, pattern)


def solution(mesh):
    placed = (P("row", None, "col", None), P("row", None))
    body = functools.partial(shards, mesh.shape["row"], mesh.shape["col"])
    return jax.shard_map(
        body, mesh=mesh, in_specs=placed, out_specs=P("row", None, "col", None), check_vma=False
    )
```

```python
import functools

import jax
import jax.numpy as jnp
from jax import lax
from jax.experimental import pallas as pl
from jax.experimental.pallas import tpu as pltpu
from jax.sharding import PartitionSpec as P

NZ = 7
MESH = pl.DeviceIdType.MESH


def split(x):
    hi = x.astype(jnp.bfloat16)
    return hi, (x - hi.astype(jnp.float32)).astype(jnp.bfloat16)


def dot3(lhi, llo, rhi, rlo):
    left = jnp.concatenate([lhi, lhi, llo], axis=1)
    right = jnp.concatenate([rhi, rlo, rhi], axis=0)
    return jnp.dot(left, right, preferred_element_type=jnp.float32)


def kernel(n_row, n_col, d_hbm, pat, out, *scratch):
    panels = scratch[:6]
    (d_ref, d_sem, mext, lhi, llo, rhi, rlo, sx, shi, slo, acc, rank, slots, m_send, m_recv, s_send,
     s_recv, p_send, p_recv, f_send, f_recv) = scratch[6:]
    w = d_ref.shape[2]
    band = d_ref.shape[1]
    half = (band - 1) // 2
    steps = half + 1
    nb = d_ref.shape[3]
    wide = 2 * nb
    tall = (band + 1) * w
    row = lax.axis_index("row")
    col = lax.axis_index("col")
    odd = lax.rem(row, 2)
    left = lax.rem(row + n_row - 1, n_row)
    right = lax.rem(row + 1, n_row)
    outer = left + odd * (right - left)
    mate = row + 1 - 2 * odd
    grid2 = n_col == 4
    if grid2:
        xn = col + 1 - 2 * lax.rem(col, 2)
        yn = lax.rem(col + 2, 4)
        peers = [xn, yn]
    else:
        peers = [lax.rem(col + d, n_col) for d in range(1, n_col)]

    def placed(v):
        return v + odd * (5 - 2 * v)

    def pair(q):
        return placed(2 - q if q < 3 else q)

    def own_place(q):
        late = lax.div(q, 3)
        return (1 - late) * (2 - q) + late * q

    def near_place(q):
        late = lax.div(q, 3)
        return (1 - late) * q + late * (8 - q)

    def landed_at(v):
        return lax.rem(14 - placed(v), 12)

    def faces_right(q):
        return odd if q < 3 else 1 - odd

    def nbr(q):
        return outer if q < 3 else mate

    def landed(q):
        p = 5 - pair(q)
        return lax.rem(p + 9, 12)

    barrier = pltpu.get_barrier_semaphore()
    for peer in peers:
        pl.semaphore_signal(barrier, inc=1, device_id=(row, peer), device_id_type=MESH)
    for peer in (left, right):
        pl.semaphore_signal(barrier, inc=1, device_id=(peer, col), device_id_type=MESH)

    fetch = pltpu.make_async_copy(d_hbm, d_ref, d_sem)
    fetch.start()

    @pl.loop(0, d_ref.shape[0])
    def _(r):
        count = jnp.int32(0)
        upto = []
        for edge in (0, band + 1):
            rank[r, edge] = jnp.int32(0)
            rank[r, 16 + edge] = jnp.int32(0)
        for s in range(band):
            on = pat[r, s]
            rank[r, s + 1] = jnp.minimum(count, NZ - 1)
            rank[r, 16 + s + 1] = on
            count = count + on
            upto.append(count)
        for t in range(NZ):
            place = jnp.int32(0)
            for s in range(band):
                place = place + jnp.where(upto[s] <= t, 1, 0)
            slots[r, t] = jnp.minimum(place, band - 1)

    fetch.wait()
    pl.semaphore_wait(barrier, len(peers) + 2)

    def m_copy(q):
        p = pair(q)
        return pltpu.make_async_remote_copy(
            mext.at[3 + p], mext.at[lax.rem(p + 9, 12)], m_send.at[q], m_recv.at[q],
            device_id=(nbr(q), col), device_id_type=MESH)

    def m_arrival(q):
        e = landed(q)
        return pltpu.make_async_remote_copy(
            mext.at[e], mext.at[e], m_send.at[q], m_recv.at[q],
            device_id=(nbr(q), col), device_id_type=MESH)

    def s_rows(q, to_right):
        size = band + 1 + 2 * (q % 3)
        return pl.ds(pl.multiple_of(to_right * ((2 * band - size) * w), 8), size * w)

    def s_copy(q):
        p = pair(q)
        rows = s_rows(q, faces_right(q))
        return pltpu.make_async_remote_copy(
            sx.at[3 + p, rows], sx.at[lax.rem(p + 9, 12), rows], s_send.at[q], s_recv.at[q],
            device_id=(nbr(q), col), device_id_type=MESH)

    def s_arrival(q):
        e = landed(q)
        rows = s_rows(q, 1 - faces_right(q))
        return pltpu.make_async_remote_copy(
            sx.at[e, rows], sx.at[e, rows], s_send.at[q], s_recv.at[q],
            device_id=(nbr(q), col), device_id_type=MESH)

    def p_copy(q, i, who, part):
        at = panels[q].at[who, (i + part) % 2]
        return pltpu.make_async_remote_copy(
            at, at, p_send.at[i, part, q], p_recv.at[i, part, q],
            device_id=(row, peers[i]), device_id_type=MESH)

    def f_copy(q, i, who):
        return pltpu.make_async_remote_copy(
            panels[q].at[who, i], panels[q].at[who, i], f_send.at[i, q], f_recv.at[i, q],
            device_id=(row, peers[1 - i]), device_id_type=MESH)

    def p_start(q):
        for part in range(2):
            for i in range(len(peers)):
                p_copy(q, i, col, part).start()

    def p_wait(q, part):
        for i in range(len(peers)):
            who = peers[i] if grid2 else lax.rem(col + n_col - 1 - i, n_col)
            p_copy(q, i, who, part).wait_recv()
            if grid2 and part == 0:
                f_copy(q, i, who).start()

    def pack(q):
        p = pair(q)
        for dr in range(2):
            r = 2 * p + dr
            for s in range(band):
                mext[3 + p, dr, pl.ds(NZ * w + s, 1)] = jnp.full(
                    (1, nb), pat[r, s].astype(jnp.float32))
            mext[3 + p, dr, pl.ds(NZ * w + band, 16 - band)] = jnp.zeros((16 - band, nb), jnp.float32)
            for t in range(NZ):
                x = d_ref[r, slots[r, t]]
                panels[q][col, dr, t] = x
                mext[3 + p, dr, pl.ds(t * w, w)] = x

    for q in (0, 1):
        pack(q)
        p_start(q)
    pack(2)
    for q in (2, 1, 0):
        m_copy(q).start()
    for q in (5, 4, 3):
        pack(q)
        m_copy(q).start()

    def store_left(e, blocks):
        gap = jnp.zeros((w, nb), jnp.float32)
        first = jnp.concatenate(blocks[0] + [gap], axis=0)
        second = jnp.concatenate([gap] + blocks[1], axis=0)
        for i, part in enumerate((first, second)):
            hi, lo = split(part)
            lhi[e, :, i * nb:(i + 1) * nb] = hi
            llo[e, :, i * nb:(i + 1) * nb] = lo

    def build_own(p):
        blocks = []
        for dr in range(2):
            r = 2 * p + dr
            blocks.append([d_ref[r, s] * pat[r, s].astype(jnp.float32) for s in range(band)])
        store_left(3 + p, blocks)

    def build_left(e):
        blocks = []
        for dr in range(2):
            here = [jnp.ones((1, nb), jnp.float32)]
            row_blocks = []
            for s in range(band):
                on = mext[e, dr, pl.ds(NZ * w + s, 1)]
                total = jnp.zeros((w, nb), jnp.float32)
                for t in range(max(0, s - band + NZ), min(NZ, s + 1)):
                    total = total + (here[t] * on) * mext[e, dr, pl.ds(t * w, w)]
                row_blocks.append(total)
                stay = [h * (1.0 - on) for h in here] + [jnp.zeros((1, nb), jnp.float32)]
                move = [jnp.zeros((1, nb), jnp.float32)] + [h * on for h in here]
                here = [a + b for a, b in zip(stay, move)][:NZ]
            blocks.append(row_blocks)
        store_left(e, blocks)

    @pl.loop(0, 6)
    def _(i):
        build_own(i)

    def build_right(q):
        p = pair(q)

        @pl.loop(0, steps)
        def _(m):
            for dj in range(2):
                for dr in range(2):
                    r = 2 * p + dr
                    s = 2 * m + dj - dr
                    t = rank[r, s + 1]
                    on = pat_wide(r, s)
                    x = panels[q][:, dr, t].reshape(nb, nb) * on
                    hi, lo = split(x)
                    at = (p * steps + m, pl.ds(dj * nb, nb), pl.ds(dr * nb, nb))
                    rhi[at] = hi
                    rlo[at] = lo

    def pat_wide(r, s):
        return rank[r, s + 1 + 16].astype(jnp.float32)

    def split_square(e, rows):
        hi, lo = split(sx[e, rows])
        shi[e, rows] = hi
        slo[e, rows] = lo

    def arrive(q):
        if q + 1 < 6:
            p_wait(q + 1, 0)
        if q + 3 < 6:
            p_start(q + 3)
        p_wait(q, 1)
        if grid2:
            for i in range(2):
                f_copy(q, i, 3 - col).wait_recv()
        m_arrival(2 - q if q < 3 else 8 - q).wait_recv()
        build_right(q)

    def case(index, branch):
        for q in range(6):
            pl.when(index == q)(functools.partial(branch, q))

    def third(p, e):
        m = e - p
        rows = pl.ds(pl.multiple_of((2 * half - 2 * m) * w, 16), tall)
        k = p * steps + m
        return dot3(shi[e, rows], slo[e, rows], rhi[k], rlo[k])

    def step(q):
        case(q, arrive)
        v0 = own_place(q)
        p = placed(v0)
        build_left(landed_at(near_place(q)))
        sx[3 + p] = jnp.zeros((2 * band * w, wide), jnp.float32)
        for m in range(steps):
            k = p * steps + m
            sx[3 + p, pl.ds(2 * m * w, tall)] += dot3(lhi[p + m], llo[p + m], rhi[k], rlo[k])
        case(q, lambda i: s_copy(i).start())
        split_square(3 + p, slice(None))
        acc[p] += third(p, 3 + p)
        late = lax.div(q, 3)
        low = (1 - late) * (v0 + 1) + late * (q - 3)
        high = (1 - late) * 3 + late * q

        @pl.loop(low, high)
        def _(v):
            pv = placed(v)
            a, b = third(p, 3 + pv), third(pv, 3 + p)
            acc[p] += a
            acc[pv] += b

    def halo_in(q):
        s_arrival(q).wait_recv()
        split_square(landed(q), s_rows(q, 1 - faces_right(q)))

    def halo_step(q):
        case(q, halo_in)
        late = lax.div(q, 3)
        e = landed_at(own_place(q))
        a = q - 3 * late

        @pl.loop(late * (5 - a), late * 6 + (1 - late) * (a + 1))
        def _(v):
            p = placed(v)
            acc[p] += third(p, e)

    acc[...] = jnp.zeros_like(acc)

    p_wait(0, 0)
    p_start(2)
    pl.loop(0, 6)(step)
    pl.loop(0, 6)(halo_step)

    @pl.loop(0, 6)
    def _(p):
        for dr in range(2):
            r = 2 * p + dr
            for i in range(band):
                lanes = pl.ds(dr * nb, nb)
                core = sx[3 + p, pl.ds((half + dr + i) * w, w), lanes]
                cube = acc[p, pl.ds((dr + i) * w, w), lanes]
                out[r, i] = (3.0 * core - 2.0 * cube) * pat[r, i].astype(jnp.float32)

    for q in range(6):
        m_copy(q).wait_send()
        s_copy(q).wait_send()
        for i in range(len(peers)):
            for part in range(2):
                p_copy(q, i, col, part).wait_send()
        if grid2:
            for i in range(2):
                f_copy(q, i, peers[i]).wait_send()


def shards(n_row, n_col, density, pattern):
    rows, band, w, nb = density.shape
    steps = (band + 1) // 2
    peers = 2 if n_col == 4 else n_col - 1
    tall, wide = (band + 1) * w, 2 * nb
    vmem, smem = pl.BlockSpec(memory_space=pltpu.VMEM), pl.BlockSpec(memory_space=pltpu.SMEM)
    f32, bf16, dma = jnp.float32, jnp.bfloat16, pltpu.SemaphoreType.DMA
    scratch = [pltpu.VMEM((n_col, 2, NZ, w, nb), f32) for _ in range(6)] + [
        pltpu.VMEM(density.shape, f32),
        dma,
        pltpu.VMEM((12, 2, NZ * w + 16, nb), f32),
        pltpu.VMEM((12, tall, wide), bf16),
        pltpu.VMEM((12, tall, wide), bf16),
        pltpu.VMEM((6 * steps, wide, wide), bf16),
        pltpu.VMEM((6 * steps, wide, wide), bf16),
        pltpu.VMEM((12, 2 * band * w, wide), f32),
        pltpu.VMEM((12, 2 * band * w, wide), bf16),
        pltpu.VMEM((12, 2 * band * w, wide), bf16),
        pltpu.VMEM((6, tall, wide), f32),
        pltpu.SMEM((rows, 32), jnp.int32),
        pltpu.SMEM((rows, 8), jnp.int32),
        dma((6,)), dma((6,)), dma((6,)), dma((6,)),
        dma((peers, 2, 6)), dma((peers, 2, 6)), dma((2, 6)), dma((2, 6)),
    ]
    return pl.pallas_call(
        functools.partial(kernel, n_row, n_col),
        out_shape=pltpu.VMEM(density.shape, f32),
        in_specs=[pl.BlockSpec(memory_space=pl.ANY), smem],
        out_specs=vmem,
        scratch_shapes=scratch,
        compiler_params=pltpu.CompilerParams(
            collective_id=0, has_side_effects=True, vmem_limit_bytes=60 * 2**20),
        name="purify",
    )(density, pattern)


def solution(mesh):
    placed = (P("row", None, "col", None), P("row", None))
    body = functools.partial(shards, mesh.shape["row"], mesh.shape["col"])
    return jax.shard_map(
        body, mesh=mesh, in_specs=placed, out_specs=P("row", None, "col", None), check_vma=False
    )
```

```python
import functools

import jax
import jax.numpy as jnp
from jax import lax
from jax.experimental import pallas as pl
from jax.experimental.pallas import tpu as pltpu
from jax.sharding import PartitionSpec as P

NZ = 7
MESH = pl.DeviceIdType.MESH


def split(x):
    hi = x.astype(jnp.bfloat16)
    return hi, (x - hi.astype(jnp.float32)).astype(jnp.bfloat16)


def dot3(lhi, llo, rhi, rlo):
    left = jnp.concatenate([lhi, lhi, llo], axis=1)
    right = jnp.concatenate([rhi, rlo, rhi], axis=0)
    return jnp.dot(left, right, preferred_element_type=jnp.float32)


def kernel(n_row, n_col, d_hbm, pat, out, *scratch):
    panels = scratch[:6]
    (d_ref, d_sem, mext, lhi, llo, rhi, rlo, sx, shi, slo, acc, rank, slots, m_send, m_recv, s_send,
     s_recv, p_send, p_recv, f_send, f_recv) = scratch[6:]
    w = d_ref.shape[2]
    band = d_ref.shape[1]
    half = (band - 1) // 2
    steps = half + 1
    nb = d_ref.shape[3]
    wide = 2 * nb
    tall = (band + 1) * w
    row = lax.axis_index("row")
    col = lax.axis_index("col")
    odd = lax.rem(row, 2)
    left = lax.rem(row + n_row - 1, n_row)
    right = lax.rem(row + 1, n_row)
    outer = left + odd * (right - left)
    mate = row + 1 - 2 * odd
    grid2 = n_col == 4
    if grid2:
        xn = col + 1 - 2 * lax.rem(col, 2)
        yn = lax.rem(col + 2, 4)
        peers = [xn, yn]
    else:
        peers = [lax.rem(col + d, n_col) for d in range(1, n_col)]

    def placed(v):
        return v + odd * (5 - 2 * v)

    def pair(q):
        return placed(2 - q if q < 3 else q)

    def own_place(q):
        late = lax.div(q, 3)
        return (1 - late) * (2 - q) + late * q

    def near_place(q):
        late = lax.div(q, 3)
        return (1 - late) * q + late * (8 - q)

    def landed_at(v):
        return lax.rem(14 - placed(v), 12)

    def faces_right(q):
        return odd if q < 3 else 1 - odd

    def nbr(q):
        return outer if q < 3 else mate

    def landed(q):
        p = 5 - pair(q)
        return lax.rem(p + 9, 12)

    barrier = pltpu.get_barrier_semaphore()
    for peer in peers:
        pl.semaphore_signal(barrier, inc=1, device_id=(row, peer), device_id_type=MESH)
    for peer in (left, right):
        pl.semaphore_signal(barrier, inc=1, device_id=(peer, col), device_id_type=MESH)

    fetch = pltpu.make_async_copy(d_hbm, d_ref, d_sem)
    fetch.start()

    fetch.wait()
    pl.semaphore_wait(barrier, len(peers) + 2)

    def m_copy(q):
        p = pair(q)
        return pltpu.make_async_remote_copy(
            mext.at[3 + p], mext.at[lax.rem(p + 9, 12)], m_send.at[q], m_recv.at[q],
            device_id=(nbr(q), col), device_id_type=MESH)

    def m_arrival(q):
        e = landed(q)
        return pltpu.make_async_remote_copy(
            mext.at[e], mext.at[e], m_send.at[q], m_recv.at[q],
            device_id=(nbr(q), col), device_id_type=MESH)

    def s_rows(q, to_right):
        size = band + 1 + 2 * (q % 3)
        return pl.ds(pl.multiple_of(to_right * ((2 * band - size) * w), 8), size * w)

    def s_copy(q):
        p = pair(q)
        rows = s_rows(q, faces_right(q))
        return pltpu.make_async_remote_copy(
            sx.at[3 + p, rows], sx.at[lax.rem(p + 9, 12), rows], s_send.at[q], s_recv.at[q],
            device_id=(nbr(q), col), device_id_type=MESH)

    def s_arrival(q):
        e = landed(q)
        rows = s_rows(q, 1 - faces_right(q))
        return pltpu.make_async_remote_copy(
            sx.at[e, rows], sx.at[e, rows], s_send.at[q], s_recv.at[q],
            device_id=(nbr(q), col), device_id_type=MESH)

    def p_copy(q, i, who, part):
        at = panels[q].at[who, (i + part) % 2]
        return pltpu.make_async_remote_copy(
            at, at, p_send.at[i, part, q], p_recv.at[i, part, q],
            device_id=(row, peers[i]), device_id_type=MESH)

    def f_copy(q, i, who):
        return pltpu.make_async_remote_copy(
            panels[q].at[who, i], panels[q].at[who, i], f_send.at[i, q], f_recv.at[i, q],
            device_id=(row, peers[1 - i]), device_id_type=MESH)

    def p_start(q):
        for part in range(2):
            for i in range(len(peers)):
                p_copy(q, i, col, part).start()

    def p_wait(q, part):
        for i in range(len(peers)):
            who = peers[i] if grid2 else lax.rem(col + n_col - 1 - i, n_col)
            p_copy(q, i, who, part).wait_recv()
            if grid2 and part == 0:
                f_copy(q, i, who).start()

    def tables(r):
        count = jnp.int32(0)
        upto = []
        for edge in (0, band + 1):
            rank[r, edge] = jnp.int32(0)
            rank[r, 16 + edge] = jnp.int32(0)
        for s in range(band):
            on = pat[r, s]
            rank[r, s + 1] = jnp.minimum(count, NZ - 1)
            rank[r, 16 + s + 1] = on
            count = count + on
            upto.append(count)
        for t in range(NZ):
            place = jnp.int32(0)
            for s in range(band):
                place = place + jnp.where(upto[s] <= t, 1, 0)
            slots[r, t] = jnp.minimum(place, band - 1)

    def pack(q):
        pl.loop(2 * pair(q), 2 * pair(q) + 2)(tables)
        p = pair(q)
        for dr in range(2):
            r = 2 * p + dr
            for s in range(band):
                mext[3 + p, dr, pl.ds(NZ * w + s, 1)] = jnp.full(
                    (1, nb), pat[r, s].astype(jnp.float32))
            mext[3 + p, dr, pl.ds(NZ * w + band, 16 - band)] = jnp.zeros((16 - band, nb), jnp.float32)
            for t in range(NZ):
                x = d_ref[r, slots[r, t]]
                panels[q][col, dr, t] = x
                mext[3 + p, dr, pl.ds(t * w, w)] = x

    for q in (0, 1):
        pack(q)
        p_start(q)
    pack(2)
    for q in (2, 1, 0):
        m_copy(q).start()
    for q in (5, 4, 3):
        pack(q)
        m_copy(q).start()

    def store_left(e, blocks):
        gap = jnp.zeros((w, nb), jnp.float32)
        first = jnp.concatenate(blocks[0] + [gap], axis=0)
        second = jnp.concatenate([gap] + blocks[1], axis=0)
        for i, part in enumerate((first, second)):
            hi, lo = split(part)
            lhi[e, :, i * nb:(i + 1) * nb] = hi
            llo[e, :, i * nb:(i + 1) * nb] = lo

    def build_own(p):
        blocks = []
        for dr in range(2):
            r = 2 * p + dr
            blocks.append([d_ref[r, s] * pat[r, s].astype(jnp.float32) for s in range(band)])
        store_left(3 + p, blocks)

    def build_left(e):
        blocks = []
        for dr in range(2):
            here = [jnp.ones((1, nb), jnp.float32)]
            row_blocks = []
            for s in range(band):
                on = mext[e, dr, pl.ds(NZ * w + s, 1)]
                total = jnp.zeros((w, nb), jnp.float32)
                for t in range(max(0, s - band + NZ), min(NZ, s + 1)):
                    total = total + (here[t] * on) * mext[e, dr, pl.ds(t * w, w)]
                row_blocks.append(total)
                stay = [h * (1.0 - on) for h in here] + [jnp.zeros((1, nb), jnp.float32)]
                move = [jnp.zeros((1, nb), jnp.float32)] + [h * on for h in here]
                here = [a + b for a, b in zip(stay, move)][:NZ]
            blocks.append(row_blocks)
        store_left(e, blocks)

    @pl.loop(0, 6)
    def _(i):
        build_own(i)

    def build_right(q):
        p = pair(q)

        @pl.loop(0, steps)
        def _(m):
            for dj in range(2):
                for dr in range(2):
                    r = 2 * p + dr
                    s = 2 * m + dj - dr
                    t = rank[r, s + 1]
                    on = pat_wide(r, s)
                    x = panels[q][:, dr, t].reshape(nb, nb) * on
                    hi, lo = split(x)
                    at = (p * steps + m, pl.ds(dj * nb, nb), pl.ds(dr * nb, nb))
                    rhi[at] = hi
                    rlo[at] = lo

    def pat_wide(r, s):
        return rank[r, s + 1 + 16].astype(jnp.float32)

    def split_square(e, rows):
        hi, lo = split(sx[e, rows])
        shi[e, rows] = hi
        slo[e, rows] = lo

    def arrive(q):
        if q + 1 < 5:
            p_wait(q + 1, 0)
        if q + 3 < 5:
            p_start(q + 3)
        if q == 3:
            p_start(5)
        p_wait(q, 1)
        if grid2:
            for i in range(2):
                f_copy(q, i, 3 - col).wait_recv()
        m_arrival(2 - q if q < 3 else 8 - q).wait_recv()
        build_right(q)

    def case(index, branch):
        for q in range(6):
            pl.when(index == q)(functools.partial(branch, q))

    def third(p, e):
        m = e - p
        rows = pl.ds(pl.multiple_of((2 * half - 2 * m) * w, 16), tall)
        k = p * steps + m
        return dot3(shi[e, rows], slo[e, rows], rhi[k], rlo[k])

    def leave(q):
        s_copy(q).start()
        if q == 4:
            p_wait(5, 0)

    def step(q):
        pl.when(q == 4)(lambda: pl.loop(0, 3)(halo_step))
        case(q, arrive)
        v0 = own_place(q)
        p = placed(v0)
        build_left(landed_at(near_place(q)))
        sx[3 + p] = jnp.zeros((2 * band * w, wide), jnp.float32)
        for m in range(steps):
            k = p * steps + m
            sx[3 + p, pl.ds(2 * m * w, tall)] += dot3(lhi[p + m], llo[p + m], rhi[k], rlo[k])
        case(q, leave)
        split_square(3 + p, slice(None))
        acc[p] += third(p, 3 + p)
        late = lax.div(q, 3)
        low = (1 - late) * (v0 + 1) + late * (q - 3)
        high = (1 - late) * 3 + late * q

        @pl.loop(low, high)
        def _(v):
            pv = placed(v)
            a, b = third(p, 3 + pv), third(pv, 3 + p)
            acc[p] += a
            acc[pv] += b

    def halo_in(q):
        s_arrival(q).wait_recv()
        split_square(landed(q), s_rows(q, 1 - faces_right(q)))

    def halo_step(q):
        case(q, halo_in)
        late = lax.div(q, 3)
        e = landed_at(own_place(q))
        a = q - 3 * late

        @pl.loop(late * (5 - a), late * 6 + (1 - late) * (a + 1))
        def _(v):
            p = placed(v)
            acc[p] += third(p, e)

    acc[...] = jnp.zeros_like(acc)

    p_wait(0, 0)
    p_start(2)
    pl.loop(0, 6)(step)
    pl.loop(3, 6)(halo_step)

    @pl.loop(0, 6)
    def _(p):
        for dr in range(2):
            r = 2 * p + dr
            for i in range(band):
                lanes = pl.ds(dr * nb, nb)
                core = sx[3 + p, pl.ds((half + dr + i) * w, w), lanes]
                cube = acc[p, pl.ds((dr + i) * w, w), lanes]
                out[r, i] = (3.0 * core - 2.0 * cube) * pat[r, i].astype(jnp.float32)

    for q in range(6):
        m_copy(q).wait_send()
        s_copy(q).wait_send()
        for i in range(len(peers)):
            for part in range(2):
                p_copy(q, i, col, part).wait_send()
        if grid2:
            for i in range(2):
                f_copy(q, i, peers[i]).wait_send()


def shards(n_row, n_col, density, pattern):
    rows, band, w, nb = density.shape
    steps = (band + 1) // 2
    peers = 2 if n_col == 4 else n_col - 1
    tall, wide = (band + 1) * w, 2 * nb
    vmem, smem = pl.BlockSpec(memory_space=pltpu.VMEM), pl.BlockSpec(memory_space=pltpu.SMEM)
    f32, bf16, dma = jnp.float32, jnp.bfloat16, pltpu.SemaphoreType.DMA
    scratch = [pltpu.VMEM((n_col, 2, NZ, w, nb), f32) for _ in range(6)] + [
        pltpu.VMEM(density.shape, f32),
        dma,
        pltpu.VMEM((12, 2, NZ * w + 16, nb), f32),
        pltpu.VMEM((12, tall, wide), bf16),
        pltpu.VMEM((12, tall, wide), bf16),
        pltpu.VMEM((6 * steps, wide, wide), bf16),
        pltpu.VMEM((6 * steps, wide, wide), bf16),
        pltpu.VMEM((12, 2 * band * w, wide), f32),
        pltpu.VMEM((12, 2 * band * w, wide), bf16),
        pltpu.VMEM((12, 2 * band * w, wide), bf16),
        pltpu.VMEM((6, tall, wide), f32),
        pltpu.SMEM((rows, 32), jnp.int32),
        pltpu.SMEM((rows, 8), jnp.int32),
        dma((6,)), dma((6,)), dma((6,)), dma((6,)),
        dma((peers, 2, 6)), dma((peers, 2, 6)), dma((2, 6)), dma((2, 6)),
    ]
    return pl.pallas_call(
        functools.partial(kernel, n_row, n_col),
        out_shape=pltpu.VMEM(density.shape, f32),
        in_specs=[pl.BlockSpec(memory_space=pl.ANY), smem],
        out_specs=vmem,
        scratch_shapes=scratch,
        compiler_params=pltpu.CompilerParams(
            collective_id=0, has_side_effects=True, vmem_limit_bytes=60 * 2**20),
        name="purify",
    )(density, pattern)


def solution(mesh):
    placed = (P("row", None, "col", None), P("row", None))
    body = functools.partial(shards, mesh.shape["row"], mesh.shape["col"])
    return jax.shard_map(
        body, mesh=mesh, in_specs=placed, out_specs=P("row", None, "col", None), check_vma=False
    )
```

```python
import functools

import jax
import jax.numpy as jnp
from jax import lax
from jax.experimental import pallas as pl
from jax.experimental.pallas import tpu as pltpu
from jax.sharding import PartitionSpec as P

NZ = 7
MESH = pl.DeviceIdType.MESH


def split(x):
    hi = x.astype(jnp.bfloat16)
    return hi, (x - hi.astype(jnp.float32)).astype(jnp.bfloat16)


def dot3(lhi, llo, rhi, rlo):
    left = jnp.concatenate([lhi, lhi, llo], axis=1)
    right = jnp.concatenate([rhi, rlo, rhi], axis=0)
    return jnp.dot(left, right, preferred_element_type=jnp.float32)


def kernel(n_row, n_col, d_hbm, pat, out, *scratch):
    panels = scratch[:6]
    (d_ref, d_sem, mext, lhi, llo, rhi, rlo, sx, shi, slo, acc, rank, slots, m_send, m_recv, s_send,
     s_recv, p_send, p_recv, f_send, f_recv) = scratch[6:]
    w = d_ref.shape[2]
    band = d_ref.shape[1]
    half = (band - 1) // 2
    steps = half + 1
    nb = d_ref.shape[3]
    wide = 2 * nb
    tall = (band + 1) * w
    row = lax.axis_index("row")
    col = lax.axis_index("col")
    odd = lax.rem(row, 2)
    left = lax.rem(row + n_row - 1, n_row)
    right = lax.rem(row + 1, n_row)
    outer = left + odd * (right - left)
    mate = row + 1 - 2 * odd
    grid2 = n_col == 4
    if grid2:
        xn = col + 1 - 2 * lax.rem(col, 2)
        yn = lax.rem(col + 2, 4)
        peers = [xn, yn]
    else:
        peers = [lax.rem(col + d, n_col) for d in range(1, n_col)]

    def placed(v):
        return v + odd * (5 - 2 * v)

    def pair(q):
        return placed(2 - q if q < 3 else q)

    def own_place(q):
        late = lax.div(q, 3)
        return (1 - late) * (2 - q) + late * q

    def near_place(q):
        late = lax.div(q, 3)
        return (1 - late) * q + late * (8 - q)

    def landed_at(v):
        return lax.rem(14 - placed(v), 12)

    def faces_right(q):
        return odd if q < 3 else 1 - odd

    def nbr(q):
        return outer if q < 3 else mate

    def landed(q):
        p = 5 - pair(q)
        return lax.rem(p + 9, 12)

    barrier = pltpu.get_barrier_semaphore()
    for peer in peers:
        pl.semaphore_signal(barrier, inc=1, device_id=(row, peer), device_id_type=MESH)
    for peer in (left, right):
        pl.semaphore_signal(barrier, inc=1, device_id=(peer, col), device_id_type=MESH)

    fetch = pltpu.make_async_copy(d_hbm, d_ref, d_sem)
    fetch.start()

    fetch.wait()
    pl.semaphore_wait(barrier, len(peers) + 2)

    def m_copy(q):
        p = pair(q)
        return pltpu.make_async_remote_copy(
            mext.at[3 + p], mext.at[lax.rem(p + 9, 12)], m_send.at[q], m_recv.at[q],
            device_id=(nbr(q), col), device_id_type=MESH)

    def m_arrival(q):
        e = landed(q)
        return pltpu.make_async_remote_copy(
            mext.at[e], mext.at[e], m_send.at[q], m_recv.at[q],
            device_id=(nbr(q), col), device_id_type=MESH)

    def s_rows(q, to_right):
        size = band + 1 + 2 * (q % 3)
        return pl.ds(pl.multiple_of(to_right * ((2 * band - size) * w), 8), size * w)

    def s_copy(q):
        p = pair(q)
        rows = s_rows(q, faces_right(q))
        return pltpu.make_async_remote_copy(
            sx.at[3 + p, rows], sx.at[lax.rem(p + 9, 12), rows], s_send.at[q], s_recv.at[q],
            device_id=(nbr(q), col), device_id_type=MESH)

    def s_arrival(q):
        e = landed(q)
        rows = s_rows(q, 1 - faces_right(q))
        return pltpu.make_async_remote_copy(
            sx.at[e, rows], sx.at[e, rows], s_send.at[q], s_recv.at[q],
            device_id=(nbr(q), col), device_id_type=MESH)

    def p_copy(q, i, who, part):
        at = panels[q].at[who, (i + part) % 2]
        return pltpu.make_async_remote_copy(
            at, at, p_send.at[i, part, q], p_recv.at[i, part, q],
            device_id=(row, peers[i]), device_id_type=MESH)

    def f_copy(q, i, who):
        return pltpu.make_async_remote_copy(
            panels[q].at[who, i], panels[q].at[who, i], f_send.at[i, q], f_recv.at[i, q],
            device_id=(row, peers[1 - i]), device_id_type=MESH)

    def p_start(q):
        for part in range(2):
            for i in range(len(peers)):
                p_copy(q, i, col, part).start()

    def p_wait(q, part):
        for i in range(len(peers)):
            who = peers[i] if grid2 else lax.rem(col + n_col - 1 - i, n_col)
            p_copy(q, i, who, part).wait_recv()
            if grid2 and part == 0:
                f_copy(q, i, who).start()

    def tables(r):
        count = jnp.int32(0)
        upto = []
        for edge in (0, band + 1):
            rank[r, edge] = jnp.int32(0)
            rank[r, 16 + edge] = jnp.int32(0)
        for s in range(band):
            on = pat[r, s]
            rank[r, s + 1] = jnp.minimum(count, NZ - 1)
            rank[r, 16 + s + 1] = on
            count = count + on
            upto.append(count)
        for t in range(NZ):
            place = jnp.int32(0)
            for s in range(band):
                place = place + jnp.where(upto[s] <= t, 1, 0)
            slots[r, t] = jnp.minimum(place, band - 1)

    def pack(q):
        pl.loop(2 * pair(q), 2 * pair(q) + 2)(tables)
        p = pair(q)
        for dr in range(2):
            r = 2 * p + dr
            for s in range(band):
                mext[3 + p, dr, pl.ds(NZ * w + s, 1)] = jnp.full(
                    (1, nb), pat[r, s].astype(jnp.float32))
            mext[3 + p, dr, pl.ds(NZ * w + band, 16 - band)] = jnp.zeros((16 - band, nb), jnp.float32)
            for t in range(NZ):
                x = d_ref[r, slots[r, t]]
                panels[q][col, dr, t] = x
                mext[3 + p, dr, pl.ds(t * w, w)] = x

    pack(2)
    m_copy(2).start()
    for q in (0, 1):
        pack(q)
        p_start(q)
    for q in (1, 0):
        m_copy(q).start()
    for q in (5, 4, 3):
        pack(q)
        m_copy(q).start()

    def store_left(e, blocks):
        gap = jnp.zeros((w, nb), jnp.float32)
        first = jnp.concatenate(blocks[0] + [gap], axis=0)
        second = jnp.concatenate([gap] + blocks[1], axis=0)
        for i, part in enumerate((first, second)):
            hi, lo = split(part)
            lhi[e, :, i * nb:(i + 1) * nb] = hi
            llo[e, :, i * nb:(i + 1) * nb] = lo

    def build_own(p):
        blocks = []
        for dr in range(2):
            r = 2 * p + dr
            blocks.append([d_ref[r, s] * pat[r, s].astype(jnp.float32) for s in range(band)])
        store_left(3 + p, blocks)

    def build_left(e):
        blocks = []
        for dr in range(2):
            here = [jnp.ones((1, nb), jnp.float32)]
            row_blocks = []
            for s in range(band):
                on = mext[e, dr, pl.ds(NZ * w + s, 1)]
                total = jnp.zeros((w, nb), jnp.float32)
                for t in range(max(0, s - band + NZ), min(NZ, s + 1)):
                    total = total + (here[t] * on) * mext[e, dr, pl.ds(t * w, w)]
                row_blocks.append(total)
                stay = [h * (1.0 - on) for h in here] + [jnp.zeros((1, nb), jnp.float32)]
                move = [jnp.zeros((1, nb), jnp.float32)] + [h * on for h in here]
                here = [a + b for a, b in zip(stay, move)][:NZ]
            blocks.append(row_blocks)
        store_left(e, blocks)

    @pl.loop(0, 6)
    def _(i):
        build_own(i)

    def build_right(q):
        p = pair(q)

        @pl.loop(0, steps)
        def _(m):
            for dj in range(2):
                for dr in range(2):
                    r = 2 * p + dr
                    s = 2 * m + dj - dr
                    t = rank[r, s + 1]
                    on = pat_wide(r, s)
                    x = panels[q][:, dr, t].reshape(nb, nb) * on
                    hi, lo = split(x)
                    at = (p * steps + m, pl.ds(dj * nb, nb), pl.ds(dr * nb, nb))
                    rhi[at] = hi
                    rlo[at] = lo

    def pat_wide(r, s):
        return rank[r, s + 1 + 16].astype(jnp.float32)

    def split_square(e, rows):
        hi, lo = split(sx[e, rows])
        shi[e, rows] = hi
        slo[e, rows] = lo

    def pass_on(q):
        if q + 1 < 6:
            p_wait(q + 1, 0)
        if q + 3 < 5:
            p_start(q + 3)
        if q == 3:
            p_start(5)

    def arrive(q):
        if q not in (0, 4):
            pass_on(q)
        p_wait(q, 1)
        if grid2:
            for i in range(2):
                f_copy(q, i, 3 - col).wait_recv()
        m_arrival(2 - q if q < 3 else 8 - q).wait_recv()
        build_right(q)

    def case(index, branch):
        for q in range(6):
            pl.when(index == q)(functools.partial(branch, q))

    def third(p, e):
        m = e - p
        rows = pl.ds(pl.multiple_of((2 * half - 2 * m) * w, 16), tall)
        k = p * steps + m
        return dot3(shi[e, rows], slo[e, rows], rhi[k], rlo[k])

    def leave(q):
        s_copy(q).start()
        if q in (0, 4):
            pass_on(q)

    def step(q):
        case(q, arrive)
        v0 = own_place(q)
        p = placed(v0)
        build_left(landed_at(near_place(q)))
        sx[3 + p] = jnp.zeros((2 * band * w, wide), jnp.float32)
        for m in range(steps):
            k = p * steps + m
            sx[3 + p, pl.ds(2 * m * w, tall)] += dot3(lhi[p + m], llo[p + m], rhi[k], rlo[k])
        case(q, leave)
        split_square(3 + p, slice(None))
        acc[p] += third(p, 3 + p)
        late = lax.div(q, 3)
        low = (1 - late) * (v0 + 1) + late * (q - 3)
        high = (1 - late) * 3 + late * q

        @pl.loop(low, high)
        def _(v):
            pv = placed(v)
            a, b = third(p, 3 + pv), third(pv, 3 + p)
            acc[p] += a
            acc[pv] += b

    def halo_in(q):
        s_arrival(q).wait_recv()
        split_square(landed(q), s_rows(q, 1 - faces_right(q)))

    def halo_step(q):
        case(q, halo_in)
        late = lax.div(q, 3)
        e = landed_at(own_place(q))
        a = q - 3 * late

        @pl.loop(late * (5 - a), late * 6 + (1 - late) * (a + 1))
        def _(v):
            p = placed(v)
            acc[p] += third(p, e)

    acc[...] = jnp.zeros_like(acc)

    p_wait(0, 0)
    p_start(2)
    pl.loop(0, 6)(step)
    pl.loop(0, 5)(lambda i: halo_step(i + lax.div(i + 1, 3)))

    def finish(v):
        p = placed(v)
        for dr in range(2):
            r = 2 * p + dr
            for i in range(band):
                lanes = pl.ds(dr * nb, nb)
                core = sx[3 + p, pl.ds((half + dr + i) * w, w), lanes]
                cube = acc[p, pl.ds((dr + i) * w, w), lanes]
                out[r, i] = (3.0 * core - 2.0 * cube) * pat[r, i].astype(jnp.float32)

    pl.loop(3, 6)(finish)
    pl.loop(2, 3)(halo_step)
    pl.loop(0, 3)(finish)

    for q in range(6):
        m_copy(q).wait_send()
        s_copy(q).wait_send()
        for i in range(len(peers)):
            for part in range(2):
                p_copy(q, i, col, part).wait_send()
        if grid2:
            for i in range(2):
                f_copy(q, i, peers[i]).wait_send()


def shards(n_row, n_col, density, pattern):
    rows, band, w, nb = density.shape
    steps = (band + 1) // 2
    peers = 2 if n_col == 4 else n_col - 1
    tall, wide = (band + 1) * w, 2 * nb
    vmem, smem = pl.BlockSpec(memory_space=pltpu.VMEM), pl.BlockSpec(memory_space=pltpu.SMEM)
    f32, bf16, dma = jnp.float32, jnp.bfloat16, pltpu.SemaphoreType.DMA
    scratch = [pltpu.VMEM((n_col, 2, NZ, w, nb), f32) for _ in range(6)] + [
        pltpu.VMEM(density.shape, f32),
        dma,
        pltpu.VMEM((12, 2, NZ * w + 16, nb), f32),
        pltpu.VMEM((12, tall, wide), bf16),
        pltpu.VMEM((12, tall, wide), bf16),
        pltpu.VMEM((6 * steps, wide, wide), bf16),
        pltpu.VMEM((6 * steps, wide, wide), bf16),
        pltpu.VMEM((12, 2 * band * w, wide), f32),
        pltpu.VMEM((12, 2 * band * w, wide), bf16),
        pltpu.VMEM((12, 2 * band * w, wide), bf16),
        pltpu.VMEM((6, tall, wide), f32),
        pltpu.SMEM((rows, 32), jnp.int32),
        pltpu.SMEM((rows, 8), jnp.int32),
        dma((6,)), dma((6,)), dma((6,)), dma((6,)),
        dma((peers, 2, 6)), dma((peers, 2, 6)), dma((2, 6)), dma((2, 6)),
    ]
    return pl.pallas_call(
        functools.partial(kernel, n_row, n_col),
        out_shape=pltpu.VMEM(density.shape, f32),
        in_specs=[pl.BlockSpec(memory_space=pl.ANY), smem],
        out_specs=vmem,
        scratch_shapes=scratch,
        compiler_params=pltpu.CompilerParams(
            collective_id=0, has_side_effects=True, vmem_limit_bytes=60 * 2**20),
        name="purify",
    )(density, pattern)


def solution(mesh):
    placed = (P("row", None, "col", None), P("row", None))
    body = functools.partial(shards, mesh.shape["row"], mesh.shape["col"])
    return jax.shard_map(
        body, mesh=mesh, in_specs=placed, out_specs=P("row", None, "col", None), check_vma=False
    )
```

```python
import functools

import jax
import jax.numpy as jnp
from jax import lax
from jax.experimental import pallas as pl
from jax.experimental.pallas import tpu as pltpu
from jax.sharding import PartitionSpec as P

NZ = 7
MESH = pl.DeviceIdType.MESH


def split(x):
    hi = x.astype(jnp.bfloat16)
    return hi, (x - hi.astype(jnp.float32)).astype(jnp.bfloat16)


def dot3(lhi, llo, rhi, rlo):
    left = jnp.concatenate([lhi, lhi, llo], axis=1)
    right = jnp.concatenate([rhi, rlo, rhi], axis=0)
    return jnp.dot(left, right, preferred_element_type=jnp.float32)


def kernel(n_row, n_col, d_hbm, pat, out, *scratch):
    panels = scratch[:6]
    (d_ref, d_sem, mext, lhi, llo, rhi, rlo, sx, shi, slo, acc, rank, slots, m_send, m_recv, s_send,
     s_recv, p_send, p_recv, f_send, f_recv) = scratch[6:]
    w = d_ref.shape[2]
    band = d_ref.shape[1]
    half = (band - 1) // 2
    steps = half + 1
    nb = d_ref.shape[3]
    wide = 2 * nb
    tall = (band + 1) * w
    row = lax.axis_index("row")
    col = lax.axis_index("col")
    odd = lax.rem(row, 2)
    left = lax.rem(row + n_row - 1, n_row)
    right = lax.rem(row + 1, n_row)
    outer = left + odd * (right - left)
    mate = row + 1 - 2 * odd
    grid2 = n_col == 4
    if grid2:
        xn = col + 1 - 2 * lax.rem(col, 2)
        yn = lax.rem(col + 2, 4)
        peers = [xn, yn]
    else:
        peers = [lax.rem(col + d, n_col) for d in range(1, n_col)]

    def placed(v):
        return v + odd * (5 - 2 * v)

    def pair(q):
        return placed(2 - q if q < 3 else q)

    def own_place(q):
        late = lax.div(q, 3)
        return (1 - late) * (2 - q) + late * q

    def near_place(q):
        late = lax.div(q, 3)
        return (1 - late) * q + late * (8 - q)

    def landed_at(v):
        return lax.rem(14 - placed(v), 12)

    def faces_right(q):
        return odd if q < 3 else 1 - odd

    def nbr(q):
        return outer if q < 3 else mate

    def landed(q):
        p = 5 - pair(q)
        return lax.rem(p + 9, 12)

    barrier = pltpu.get_barrier_semaphore()
    for peer in peers:
        pl.semaphore_signal(barrier, inc=1, device_id=(row, peer), device_id_type=MESH)
    for peer in (left, right):
        pl.semaphore_signal(barrier, inc=1, device_id=(peer, col), device_id_type=MESH)

    fetch = pltpu.make_async_copy(d_hbm, d_ref, d_sem)
    fetch.start()

    fetch.wait()
    pl.semaphore_wait(barrier, len(peers) + 2)

    def m_copy(q):
        p = pair(q)
        return pltpu.make_async_remote_copy(
            mext.at[3 + p], mext.at[lax.rem(p + 9, 12)], m_send.at[q], m_recv.at[q],
            device_id=(nbr(q), col), device_id_type=MESH)

    def m_arrival(q):
        e = landed(q)
        return pltpu.make_async_remote_copy(
            mext.at[e], mext.at[e], m_send.at[q], m_recv.at[q],
            device_id=(nbr(q), col), device_id_type=MESH)

    def s_rows(q, to_right):
        size = band + 1 + 2 * (q % 3)
        return pl.ds(pl.multiple_of(to_right * ((2 * band - size) * w), 8), size * w)

    def s_copy(q):
        p = pair(q)
        rows = s_rows(q, faces_right(q))
        return pltpu.make_async_remote_copy(
            sx.at[3 + p, rows], sx.at[lax.rem(p + 9, 12), rows], s_send.at[q], s_recv.at[q],
            device_id=(nbr(q), col), device_id_type=MESH)

    def s_arrival(q):
        e = landed(q)
        rows = s_rows(q, 1 - faces_right(q))
        return pltpu.make_async_remote_copy(
            sx.at[e, rows], sx.at[e, rows], s_send.at[q], s_recv.at[q],
            device_id=(nbr(q), col), device_id_type=MESH)

    def p_copy(q, i, who, part):
        at = panels[q].at[who, (i + part) % 2]
        return pltpu.make_async_remote_copy(
            at, at, p_send.at[i, part, q], p_recv.at[i, part, q],
            device_id=(row, peers[i]), device_id_type=MESH)

    def f_copy(q, i, who):
        return pltpu.make_async_remote_copy(
            panels[q].at[who, i], panels[q].at[who, i], f_send.at[i, q], f_recv.at[i, q],
            device_id=(row, peers[1 - i]), device_id_type=MESH)

    def p_start(q):
        for part in range(2):
            for i in range(len(peers)):
                p_copy(q, i, col, part).start()

    def p_wait(q, part):
        for i in range(len(peers)):
            who = peers[i] if grid2 else lax.rem(col + n_col - 1 - i, n_col)
            p_copy(q, i, who, part).wait_recv()
            if grid2 and part == 0:
                f_copy(q, i, who).start()

    def tables(r):
        count = jnp.int32(0)
        upto = []
        for edge in (0, band + 1):
            rank[r, edge] = jnp.int32(0)
            rank[r, 16 + edge] = jnp.int32(0)
        for s in range(band):
            on = pat[r, s]
            rank[r, s + 1] = jnp.minimum(count, NZ - 1)
            rank[r, 16 + s + 1] = on
            count = count + on
            upto.append(count)
        for t in range(NZ):
            place = jnp.int32(0)
            for s in range(band):
                place = place + jnp.where(upto[s] <= t, 1, 0)
            slots[r, t] = jnp.minimum(place, band - 1)

    def pack(q):
        pl.loop(2 * pair(q), 2 * pair(q) + 2)(tables)
        p = pair(q)
        for dr in range(2):
            r = 2 * p + dr
            for s in range(band):
                mext[3 + p, dr, pl.ds(NZ * w + s, 1)] = jnp.full(
                    (1, nb), pat[r, s].astype(jnp.float32))
            mext[3 + p, dr, pl.ds(NZ * w + band, 16 - band)] = jnp.zeros((16 - band, nb), jnp.float32)
            for t in range(NZ):
                x = d_ref[r, slots[r, t]]
                panels[q][col, dr, t] = x
                mext[3 + p, dr, pl.ds(t * w, w)] = x

    pack(2)
    m_copy(2).start()
    for q in (0, 1):
        pack(q)
        p_start(q)
    for q in (1, 0):
        m_copy(q).start()
    for q in (5, 4, 3):
        pack(q)
        m_copy(q).start()

    def store_left(e, blocks):
        gap = jnp.zeros((w, nb), jnp.float32)
        first = jnp.concatenate(blocks[0] + [gap], axis=0)
        second = jnp.concatenate([gap] + blocks[1], axis=0)
        for i, part in enumerate((first, second)):
            hi, lo = split(part)
            lhi[e, :, i * nb:(i + 1) * nb] = hi
            llo[e, :, i * nb:(i + 1) * nb] = lo

    def build_own(p):
        blocks = []
        for dr in range(2):
            r = 2 * p + dr
            blocks.append([d_ref[r, s] * pat[r, s].astype(jnp.float32) for s in range(band)])
        store_left(3 + p, blocks)

    def build_left(e):
        blocks = []
        for dr in range(2):
            here = [jnp.ones((1, nb), jnp.float32)]
            row_blocks = []
            for s in range(band):
                on = mext[e, dr, pl.ds(NZ * w + s, 1)]
                total = jnp.zeros((w, nb), jnp.float32)
                for t in range(max(0, s - band + NZ), min(NZ, s + 1)):
                    total = total + (here[t] * on) * mext[e, dr, pl.ds(t * w, w)]
                row_blocks.append(total)
                stay = [h * (1.0 - on) for h in here] + [jnp.zeros((1, nb), jnp.float32)]
                move = [jnp.zeros((1, nb), jnp.float32)] + [h * on for h in here]
                here = [a + b for a, b in zip(stay, move)][:NZ]
            blocks.append(row_blocks)
        store_left(e, blocks)

    @pl.loop(0, 6)
    def _(i):
        build_own(i)

    def build_right(q):
        p = pair(q)

        @pl.loop(0, steps)
        def _(m):
            for dj in range(2):
                for dr in range(2):
                    r = 2 * p + dr
                    s = 2 * m + dj - dr
                    t = rank[r, s + 1]
                    on = pat_wide(r, s)
                    x = panels[q][:, dr, t].reshape(nb, nb) * on
                    hi, lo = split(x)
                    at = (p * steps + m, pl.ds(dj * nb, nb), pl.ds(dr * nb, nb))
                    rhi[at] = hi
                    rlo[at] = lo

    def pat_wide(r, s):
        return rank[r, s + 1 + 16].astype(jnp.float32)

    def split_square(e, rows):
        hi, lo = split(sx[e, rows])
        shi[e, rows] = hi
        slo[e, rows] = lo

    def pass_on(q):
        if q + 1 < 6:
            p_wait(q + 1, 0)
        if q + 3 < 5:
            p_start(q + 3)
        if q == 3:
            p_start(5)

    def arrive(q):
        if q not in (0, 4):
            pass_on(q)
        p_wait(q, 1)
        if grid2:
            for i in range(2):
                f_copy(q, i, 3 - col).wait_recv()
        m_arrival(2 - q if q < 3 else 8 - q).wait_recv()
        build_right(q)

    def case(index, branch):
        for q in range(6):
            pl.when(index == q)(functools.partial(branch, q))

    def third(p, e):
        m = e - p
        rows = pl.ds(pl.multiple_of((2 * half - 2 * m) * w, 16), tall)
        k = p * steps + m
        return dot3(shi[e, rows], slo[e, rows], rhi[k], rlo[k])

    def leave(q):
        s_copy(q).start()
        if q in (0, 4):
            pass_on(q)

    def step(q):
        pl.when(q == 5)(lambda: pl.loop(0, 2)(halo_step))
        case(q, arrive)
        v0 = own_place(q)
        p = placed(v0)
        build_left(landed_at(near_place(q)))
        sx[3 + p] = jnp.zeros((2 * band * w, wide), jnp.float32)
        for m in range(steps):
            k = p * steps + m
            sx[3 + p, pl.ds(2 * m * w, tall)] += dot3(lhi[p + m], llo[p + m], rhi[k], rlo[k])
        case(q, leave)
        split_square(3 + p, slice(None))
        acc[p] += third(p, 3 + p)
        late = lax.div(q, 3)
        low = (1 - late) * (v0 + 1) + late * (q - 3)
        high = (1 - late) * 3 + late * q

        @pl.loop(low, high)
        def _(v):
            pv = placed(v)
            a, b = third(p, 3 + pv), third(pv, 3 + p)
            acc[p] += a
            acc[pv] += b

    def halo_in(q):
        s_arrival(q).wait_recv()
        split_square(landed(q), s_rows(q, 1 - faces_right(q)))

    def halo_step(q):
        case(q, halo_in)
        late = lax.div(q, 3)
        e = landed_at(own_place(q))
        a = q - 3 * late

        @pl.loop(late * (5 - a), late * 6 + (1 - late) * (a + 1))
        def _(v):
            p = placed(v)
            acc[p] += third(p, e)

    acc[...] = jnp.zeros_like(acc)

    p_wait(0, 0)
    p_start(2)
    pl.loop(0, 6)(step)
    pl.loop(3, 6)(halo_step)

    def finish(v):
        p = placed(v)
        for dr in range(2):
            r = 2 * p + dr
            for i in range(band):
                lanes = pl.ds(dr * nb, nb)
                core = sx[3 + p, pl.ds((half + dr + i) * w, w), lanes]
                cube = acc[p, pl.ds((dr + i) * w, w), lanes]
                out[r, i] = (3.0 * core - 2.0 * cube) * pat[r, i].astype(jnp.float32)

    pl.loop(3, 6)(finish)
    pl.loop(2, 3)(halo_step)
    pl.loop(0, 3)(finish)

    for q in range(6):
        m_copy(q).wait_send()
        s_copy(q).wait_send()
        for i in range(len(peers)):
            for part in range(2):
                p_copy(q, i, col, part).wait_send()
        if grid2:
            for i in range(2):
                f_copy(q, i, peers[i]).wait_send()


def shards(n_row, n_col, density, pattern):
    rows, band, w, nb = density.shape
    steps = (band + 1) // 2
    peers = 2 if n_col == 4 else n_col - 1
    tall, wide = (band + 1) * w, 2 * nb
    vmem, smem = pl.BlockSpec(memory_space=pltpu.VMEM), pl.BlockSpec(memory_space=pltpu.SMEM)
    f32, bf16, dma = jnp.float32, jnp.bfloat16, pltpu.SemaphoreType.DMA
    scratch = [pltpu.VMEM((n_col, 2, NZ, w, nb), f32) for _ in range(6)] + [
        pltpu.VMEM(density.shape, f32),
        dma,
        pltpu.VMEM((12, 2, NZ * w + 16, nb), f32),
        pltpu.VMEM((12, tall, wide), bf16),
        pltpu.VMEM((12, tall, wide), bf16),
        pltpu.VMEM((6 * steps, wide, wide), bf16),
        pltpu.VMEM((6 * steps, wide, wide), bf16),
        pltpu.VMEM((12, 2 * band * w, wide), f32),
        pltpu.VMEM((12, 2 * band * w, wide), bf16),
        pltpu.VMEM((12, 2 * band * w, wide), bf16),
        pltpu.VMEM((6, tall, wide), f32),
        pltpu.SMEM((rows, 32), jnp.int32),
        pltpu.SMEM((rows, 8), jnp.int32),
        dma((6,)), dma((6,)), dma((6,)), dma((6,)),
        dma((peers, 2, 6)), dma((peers, 2, 6)), dma((2, 6)), dma((2, 6)),
    ]
    return pl.pallas_call(
        functools.partial(kernel, n_row, n_col),
        out_shape=pltpu.VMEM(density.shape, f32),
        in_specs=[pl.BlockSpec(memory_space=pl.ANY), smem],
        out_specs=vmem,
        scratch_shapes=scratch,
        compiler_params=pltpu.CompilerParams(
            collective_id=0, has_side_effects=True, vmem_limit_bytes=60 * 2**20),
        name="purify",
    )(density, pattern)


def solution(mesh):
    placed = (P("row", None, "col", None), P("row", None))
    body = functools.partial(shards, mesh.shape["row"], mesh.shape["col"])
    return jax.shard_map(
        body, mesh=mesh, in_specs=placed, out_specs=P("row", None, "col", None), check_vma=False
    )
```
